32 devices in a mesh: groups: 2 (over x), seq: 16 (over z, y, core).
Axes of the slice: x: 2, y: 2, z: 4, core: 2. Of those that a mesh axis runs over, the one named last changes fastest.
Arguments:
- queries: bfloat16 [4096, 2560], P(('groups', 'seq')), parts along dimension 0, may hold values from -6 to 6
- key_vectors: bfloat16 [4096, 2560], P(('groups', 'seq')), parts along dimension 0, may hold values from -6 to 6
- value_vectors: bfloat16 [4096, 2560], P(('groups', 'seq')), parts along dimension 0, may hold values from -6 to 6
- token_rates: float32 [4096, 20], P(('groups', 'seq')), parts along dimension 0, may hold values from 0.25 to 2.5
- fast_weights: bfloat16 [1024, 3, 20, 128], P(('groups', 'seq')), parts along dimension 0, may hold values from -4 to 4
Outputs:
- applied: bfloat16 [4096, 2560], P(('groups', 'seq')), parts along dimension 0
- renewed: bfloat16 [1024, 3, 20, 128], P(('groups', 'seq')), parts along dimension 0
The draws below stay inside these ranges and needn't reach their ends.
There are 2 independent parts, one for each index of `groups`. The reference program is written for one: setup_inputs(seed, part) draws one part's arguments, and reference() takes and returns one part's arrays. A program takes and returns all parts, laid end to end along the dimension named above; each array names one. Nothing has to cross between parts.
All inputs are finite; a program needn't handle non-finite values.
Results may differ from the reference program's by a relative error of at most 0.0049.
Values may be sent and summed in bfloat16 or wider, within the bound.
No kernel may reach another device: no remote copies, remote signals or barrier semaphores. Data moves between devices by JAX's collectives and lax.ppermute only.
A program may use at most 128 MiB of HBM per device.

```python
import math
import jax
import jax.numpy as jnp
from jax import lax

HEADS = 20
DH = 128
HID = 512
NS_STEPS = 2
TOKENS = 2048


def level_of(own_key, extent, shards, smallest, largest):
    def one(axis_at, parts):
        heights = jax.random.uniform(jax.random.fold_in(jax.random.fold_in(own_key, 6), axis_at), (parts,), jnp.float32, smallest / len(shards), largest / len(shards))
        return jnp.repeat(jnp.exp(heights), extent[axis_at] // parts).reshape((-1,) + (1,) * (len(extent) - axis_at - 1))

    factor_of = one(*shards[0])
    for cut in shards[1:]:
        factor_of = factor_of * one(*cut)
    return factor_of


def bell_draw(stream_key, extent, spread, limit, split=(), held_as=jnp.bfloat16):
    drawn = spread * jax.random.normal(stream_key, extent, jnp.float32)
    if split:
        drawn = drawn * level_of(stream_key, extent, split, -0.22, 0.18)
    return jnp.clip(drawn, -limit, limit).astype(held_as)


def setup_inputs(seed: int = 0, part: int = 0) -> dict:
    key_list = jax.random.split(jax.random.key(seed), 6)
    part_keys = jax.random.split(jax.random.fold_in(key_list[5], part), 6)
    queries = bell_draw(part_keys[0], (TOKENS, HEADS * DH), 1.0, 6.0, ((0, 16),))
    key_vectors = bell_draw(part_keys[1], (TOKENS, HEADS * DH), 1.0, 6.0, ((0, 16),))
    value_vectors = bell_draw(part_keys[2], (TOKENS, HEADS * DH), 1.0, 6.0, ((0, 16),))
    token_rates = jnp.clip(jnp.exp(math.log(2.5) - 2.3025851 * jax.random.uniform(part_keys[3], (TOKENS, HEADS), jnp.float32) ** level_of(part_keys[3], (TOKENS, HEADS), ((0, 16),), -0.2, 0.2)), 0.25, 2.5)
    fast_weights = bell_draw(part_keys[4], (HID, 3, HEADS, DH), 1.0, 4.0, ((0, 16),))
    return {"queries": queries, "key_vectors": key_vectors, "value_vectors": value_vectors, "token_rates": token_rates, "fast_weights": fast_weights}


coef_a = 3.4445
coef_b = -4.775
coef_c = 2.0315

def orthogonal_update(gradient):
    exact = lax.Precision.HIGHEST
    gram_matrix = jnp.einsum('jmd,jme->mde', gradient, gradient, precision=exact)
    trace_sum = jnp.trace(gram_matrix, axis1=1, axis2=2)
    factor = 1.0 / (jnp.sqrt(trace_sum) + 1e-07)
    poly_factor = factor[:, None, None] * jnp.eye(DH, dtype=jnp.float32)[None, :, :]
    for newton_step in range(NS_STEPS):
        inner_term = jnp.matmul(gram_matrix, poly_factor, precision=exact)
        square = jnp.matmul(poly_factor, inner_term, precision=exact)
        mixed_term = coef_b * square + coef_c * jnp.matmul(square, square, precision=exact)
        poly_factor = coef_a * poly_factor + jnp.matmul(mixed_term, poly_factor, precision=exact)
    return jnp.einsum('mde,jme->jmd', poly_factor, gradient, precision=exact)

def head_pass(inputs):
    query_rows, key_rows, value_rows, rate_rows, weights = inputs
    scale_in = 1.0 / math.sqrt(DH)
    scale_out = 1.0 / math.sqrt(HID)
    first_map = weights[:, 0, :].T
    third_map = weights[:, 1, :].T
    second = weights[:, 2, :]
    query_first = scale_in * jnp.dot(query_rows, first_map, preferred_element_type=jnp.float32)
    query_third = scale_in * jnp.dot(query_rows, third_map, preferred_element_type=jnp.float32)
    hidden_q = (query_first * jax.nn.sigmoid(query_first) * query_third).astype(jnp.bfloat16)
    applied = (scale_out * jnp.dot(hidden_q, second, preferred_element_type=jnp.float32)).astype(jnp.bfloat16)
    key_first = scale_in * jnp.dot(key_rows, first_map, preferred_element_type=jnp.float32)
    key_third = scale_in * jnp.dot(key_rows, third_map, preferred_element_type=jnp.float32)
    sigmoid_k = jax.nn.sigmoid(key_first)
    activated = key_first * sigmoid_k
    hidden_k = (activated * key_third).astype(jnp.bfloat16)
    scaled_v = (-scale_out * rate_rows[:, None] * value_rows.astype(jnp.float32)).astype(jnp.bfloat16)
    back_grad = jnp.dot(scaled_v, second.T, preferred_element_type=jnp.float32)
    grad_third = (back_grad * activated).astype(jnp.bfloat16)
    grad_first = (back_grad * key_third * sigmoid_k * (1.0 + key_first * (1.0 - sigmoid_k))).astype(jnp.bfloat16)
    grad_one = scale_in * jnp.dot(grad_first.T, key_rows, preferred_element_type=jnp.float32)
    grad_two = scale_in * jnp.dot(grad_third.T, key_rows, preferred_element_type=jnp.float32)
    grad_out = jnp.dot(hidden_k.T, scaled_v, preferred_element_type=jnp.float32)
    gradient = jnp.stack([grad_one, grad_two, grad_out], axis=1)
    update = orthogonal_update(gradient)
    renewed = (weights.astype(jnp.float32) - math.sqrt(HID) * update).astype(jnp.bfloat16)
    return (applied, renewed)

def reference(queries, key_vectors, value_vectors, token_rates, fast_weights):
    row_count = queries.shape[0]

    def split_heads(tensor):
        return tensor.reshape(row_count, HEADS, DH).transpose(1, 0, 2)
    stacked = (split_heads(queries), split_heads(key_vectors), split_heads(value_vectors), token_rates.T, fast_weights.transpose(2, 0, 1, 3))
    applied, renewed = lax.map(head_pass, stacked)
    return (applied.transpose(1, 0, 2).reshape(row_count, HEADS * DH), renewed.transpose(1, 2, 0, 3))
```

```python
import functools
import math

import jax
import jax.numpy as jnp
from jax import lax
from jax.experimental import pallas as pl
from jax.experimental.pallas import tpu as pltpu
from jax.sharding import PartitionSpec as P

HID = 512
NS_STEPS = 2
PLANE = 4

coef_a = 3.4445
coef_b = -4.775
coef_c = 2.0315

VMEM = pltpu.VMEM
SMEM = pltpu.SMEM
NT = (((1,), (1,)), ((), ()))
NN = (((1,), (0,)), ((), ()))
TN = (((0,), (0,)), ((), ()))


def dot(a, b, dims, precision=None):
    return lax.dot_general(a, b, dims, precision=precision, preferred_element_type=jnp.float32)


def key_kernel(heads, place_ref, k_ref, s_ref, w0, w1, w2, w3, keep_ref, send_ref, weights):
    place = place_ref[0]
    planes, rows, head_size = k_ref.shape
    slots = keep_ref.shape[1]
    tokens = planes * rows
    step = pl.program_id(0)
    scale_in = 1.0 / math.sqrt(head_size)
    quarter = weights.shape[1] // PLANE
    for rel, w in enumerate((w0, w1, w2, w3)):
        at = pl.multiple_of((place ^ rel) * quarter, quarter)
        for matrix in range(3):
            weights[matrix, pl.ds(at, quarter), :] = w[:, 0, matrix].reshape(quarter, head_size)
    keys = k_ref[...].reshape(tokens, head_size)
    scaled = s_ref[...].reshape(tokens, head_size)
    hid = weights.shape[1]

    @pl.when(step == 0)
    def _():
        for index in range(3 * heads, PLANE * slots):
            rel = (index // slots) ^ place
            keep_ref[rel // 2, index % slots] = jnp.zeros((hid, head_size), keep_ref.dtype)
            send_ref[rel // 2, index % slots] = jnp.zeros((hid, head_size), send_ref.dtype)

    block = 128
    for at in range(0, hid, block):
        rows_at = slice(at, at + block)
        raw_first = dot(weights[0, rows_at], keys, NT)
        raw_third = dot(weights[1, rows_at], keys, NT)
        back = dot(weights[2, rows_at], scaled, NT)
        first = raw_first * scale_in
        sig = 0.5 * jnp.tanh(0.5 * first) + 0.5
        act = first * sig
        hidden = (act * raw_third).astype(jnp.bfloat16)
        grad_third = (back * act).astype(jnp.bfloat16)
        slope = sig + act * (1.0 - sig)
        grad_first = (back * raw_third * slope).astype(jnp.bfloat16)
        terms = (
            dot(grad_first, keys, NN) * (scale_in * scale_in),
            dot(grad_third, keys, NN) * scale_in,
            dot(hidden, scaled, NN) * scale_in,
        )
        for matrix in range(3):
            index = 3 * step + matrix
            rel = (index // slots) ^ place
            slot = index % slots
            half = rel // 2

            @pl.when(rel % 2 == 0)
            def _():
                keep_ref[half, slot, rows_at, :] = terms[matrix]

            @pl.when(rel % 2 == 1)
            def _():
                send_ref[half, slot, rows_at, :] = terms[matrix].astype(send_ref.dtype)


def query_kernel(place_ref, q_ref, w0, w1, w2, w3, out_ref, weights):
    place = place_ref[0]
    planes, rows, head_size = q_ref.shape
    tokens = planes * rows
    scale_in = 1.0 / math.sqrt(head_size)
    scale_out = 1.0 / math.sqrt(HID)
    quarter = weights.shape[1] // PLANE
    for rel, w in enumerate((w0, w1, w2, w3)):
        at = pl.multiple_of((place ^ rel) * quarter, quarter)
        for matrix in range(3):
            weights[matrix, pl.ds(at, quarter), :] = w[:, 0, matrix].reshape(quarter, head_size)
    for plane in range(planes):
        queries = q_ref[plane]
        first = dot(queries, weights[0], NT) * scale_in
        third = dot(queries, weights[1], NT) * scale_in
        sig = 0.5 * jnp.tanh(0.5 * first) + 0.5
        hidden = (first * sig * third).astype(jnp.bfloat16)
        out_ref[plane] = (dot(hidden, weights[2], NN) * scale_out).astype(out_ref.dtype)


def renew_kernel(place_ref, mine_ref, got_ref, w0, w1, w2, w3, out_ref, updates):
    place = place_ref[0]
    slots, hid, head_size = mine_ref.shape
    planes, heads = w0.shape[0], w0.shape[1]
    exact = lax.Precision.HIGHEST
    quarter = hid // PLANE
    rows = quarter // planes
    eye = (
        lax.broadcasted_iota(jnp.int32, (head_size, head_size), 0)
        == lax.broadcasted_iota(jnp.int32, (head_size, head_size), 1)
    ).astype(jnp.float32)
    grads = [mine_ref[slot] + got_ref[slot].astype(jnp.float32) for slot in range(slots)]
    grams = [dot(grad, grad, TN, exact) for grad in grads]
    factors = [eye * (1.0 / (jnp.sqrt(jnp.sum(gram * eye)) + 1e-07)) for gram in grams]
    for _ in range(NS_STEPS):
        inner = [dot(gram, factor, NN, exact) for gram, factor in zip(grams, factors)]
        square = [dot(factor, term, NN, exact) for factor, term in zip(factors, inner)]
        mixed = [coef_b * term + coef_c * dot(term, term, NN, exact) for term in square]
        factors = [coef_a * factor + dot(term, factor, NN, exact) for term, factor in zip(mixed, factors)]
    for slot in range(slots):
        updates[slot] = math.sqrt(HID) * dot(grads[slot], factors[slot], NT, exact)
    for slot in range(slots):
        index = jnp.minimum(place * slots + slot, 3 * heads - 1)
        head, matrix = index // 3, index % 3
        for rel, w in enumerate((w0, w1, w2, w3)):
            spot = place ^ rel
            for plane in range(planes):
                at = pl.multiple_of(spot * quarter + plane * rows, rows)
                old = w[plane, head, matrix].astype(jnp.float32)
                out_ref[plane, spot, slot] = (old - updates[slot, pl.ds(at, rows), :]).astype(out_ref.dtype)


def plane_body(queries, key_vectors, value_vectors, token_rates, fast_weights, planes):
    row_count = queries.shape[0]
    own_rows, _, num_heads, head_size = fast_weights.shape
    heads = num_heads // planes
    width = heads * head_size
    size = planes * PLANE
    slots = -(-3 * heads // PLANE)
    scale_out = 1.0 / math.sqrt(HID)
    lines = [[PLANE * plane + spot for plane in range(planes)] for spot in range(PLANE)]
    place = (lax.axis_index("seq") % PLANE).astype(jnp.int32).reshape(1)

    def along(array):
        return lax.all_to_all(array, "seq", 0, 0, axis_index_groups=lines, tiled=True)

    def swap(array, bit):
        return lax.ppermute(array, "seq", [(at, at ^ bit) for at in range(size)])

    sent_w = fast_weights.reshape(own_rows, 3, planes, heads, head_size).transpose(2, 3, 1, 0, 4)
    w0 = along(sent_w)
    w2 = swap(w0, 2)
    w1 = swap(w0, 1)
    w3 = swap(w2, 1)
    weights = (w0, w1, w2, w3)

    scaled_v = (
        (-scale_out * token_rates[:, :, None])
        * value_vectors.reshape(row_count, num_heads, head_size).astype(jnp.float32)
    ).astype(jnp.bfloat16).reshape(row_count, num_heads * head_size)

    def split(array):
        return array.reshape(row_count, planes, width).transpose(1, 0, 2)

    keys = along(split(key_vectors))
    scaled = along(split(scaled_v))
    moved_q = along(split(queries))

    smem = pl.BlockSpec(memory_space=SMEM)
    rows_spec = pl.BlockSpec((planes, row_count, head_size), lambda h: (0, 0, h))
    weight_spec = pl.BlockSpec((planes, 1, 3, own_rows, head_size), lambda h: (0, h, 0, 0, 0))
    hid = size * own_rows
    grad_shape = (2, slots, hid, head_size)
    keep, send = pl.pallas_call(
        functools.partial(key_kernel, heads),
        grid=(heads,),
        in_specs=[smem, rows_spec, rows_spec] + [weight_spec] * 4,
        out_specs=[pl.BlockSpec(grad_shape, lambda h: (0, 0, 0, 0))] * 2,
        out_shape=[
            jax.ShapeDtypeStruct(grad_shape, jnp.float32),
            jax.ShapeDtypeStruct(grad_shape, jnp.bfloat16),
        ],
        scratch_shapes=[VMEM((3, hid, head_size), jnp.bfloat16)],
        compiler_params=pltpu.CompilerParams(vmem_limit_bytes=32 * 2**20),
        cost_estimate=pl.CostEstimate(flops=2 * 10**9, bytes_accessed=10**7, transcendentals=10**6),
        name="key_side",
    )(place, keys, scaled, *weights)

    got = swap(send, 1).astype(jnp.float32)
    mine = keep[0] + got[0]
    other = (keep[1] + got[1]).astype(jnp.bfloat16)
    last = swap(other, 2)

    renewed = pl.pallas_call(
        renew_kernel,
        in_specs=[smem] + [pl.BlockSpec(memory_space=VMEM)] * 6,
        out_specs=pl.BlockSpec(memory_space=VMEM),
        out_shape=jax.ShapeDtypeStruct((planes, PLANE, slots, own_rows, head_size), jnp.bfloat16),
        scratch_shapes=[VMEM((slots, hid, head_size), jnp.float32)],
        compiler_params=pltpu.CompilerParams(vmem_limit_bytes=32 * 2**20),
        cost_estimate=pl.CostEstimate(flops=10**9, bytes_accessed=10**7, transcendentals=0),
        name="renew",
    )(place, mine, last, *weights)
    back = lax.all_to_all(
        renewed.reshape(size, slots, own_rows, head_size), "seq", 0, 0, tiled=True
    ).reshape(planes, PLANE * slots, own_rows, head_size)[:, : 3 * heads]
    renewed_out = (
        back.reshape(planes, heads, 3, own_rows, head_size)
        .transpose(3, 2, 0, 1, 4)
        .reshape(own_rows, 3, num_heads, head_size)
    )

    moved_out = pl.pallas_call(
        query_kernel,
        grid=(heads,),
        in_specs=[smem, rows_spec] + [weight_spec] * 4,
        out_specs=rows_spec,
        out_shape=jax.ShapeDtypeStruct((planes, row_count, width), jnp.bfloat16),
        scratch_shapes=[VMEM((3, hid, head_size), jnp.bfloat16)],
        compiler_params=pltpu.CompilerParams(vmem_limit_bytes=32 * 2**20),
        cost_estimate=pl.CostEstimate(flops=10**9, bytes_accessed=10**7, transcendentals=10**6),
        name="query_side",
    )(place, moved_q, *weights)
    applied = along(moved_out).transpose(1, 0, 2).reshape(row_count, planes * width)
    return applied, renewed_out


def newton_factor(gram_matrix):
    exact = lax.Precision.HIGHEST
    head_size = gram_matrix.shape[-1]
    trace_sum = jnp.trace(gram_matrix, axis1=-2, axis2=-1)
    factor = 1.0 / (jnp.sqrt(trace_sum) + 1e-07)
    poly_factor = factor[..., None, None] * jnp.eye(head_size, dtype=jnp.float32)
    for newton_step in range(NS_STEPS):
        inner_term = jnp.matmul(gram_matrix, poly_factor, precision=exact)
        square = jnp.matmul(poly_factor, inner_term, precision=exact)
        mixed_term = coef_b * square + coef_c * jnp.matmul(square, square, precision=exact)
        poly_factor = coef_a * poly_factor + jnp.matmul(mixed_term, poly_factor, precision=exact)
    return poly_factor


def hidden_block(query_heads, key_heads, scaled_v, weight_block):
    head_size = query_heads.shape[2]
    scale_in = 1.0 / math.sqrt(head_size)
    scale_out = 1.0 / math.sqrt(HID)
    query_first = scale_in * jnp.einsum(
        "thd,jhd->thj", query_heads, weight_block[:, 0], preferred_element_type=jnp.float32
    )
    query_third = scale_in * jnp.einsum(
        "thd,jhd->thj", query_heads, weight_block[:, 1], preferred_element_type=jnp.float32
    )
    hidden_q = (query_first * jax.nn.sigmoid(query_first) * query_third).astype(jnp.bfloat16)
    partial_out = scale_out * jnp.einsum(
        "thj,jhd->thd", hidden_q, weight_block[:, 2], preferred_element_type=jnp.float32
    )
    key_first = scale_in * jnp.einsum(
        "thd,jhd->thj", key_heads, weight_block[:, 0], preferred_element_type=jnp.float32
    )
    key_third = scale_in * jnp.einsum(
        "thd,jhd->thj", key_heads, weight_block[:, 1], preferred_element_type=jnp.float32
    )
    sigmoid_k = jax.nn.sigmoid(key_first)
    activated = key_first * sigmoid_k
    hidden_k = (activated * key_third).astype(jnp.bfloat16)
    back_grad = jnp.einsum(
        "thd,jhd->thj", scaled_v, weight_block[:, 2], preferred_element_type=jnp.float32
    )
    grad_third = (back_grad * activated).astype(jnp.bfloat16)
    grad_first = (back_grad * key_third * sigmoid_k * (1.0 + key_first * (1.0 - sigmoid_k))).astype(
        jnp.bfloat16
    )
    return (partial_out, hidden_k, grad_first, grad_third)


def gather_body(queries, key_vectors, value_vectors, token_rates, fast_weights):
    exact = lax.Precision.HIGHEST
    row_count = queries.shape[0]
    num_heads = fast_weights.shape[2]
    head_size = fast_weights.shape[3]
    scale_in = 1.0 / math.sqrt(head_size)
    scale_out = 1.0 / math.sqrt(HID)
    query_heads = queries.reshape(row_count, num_heads, head_size)
    key_heads = key_vectors.reshape(row_count, num_heads, head_size)
    value_heads = value_vectors.reshape(row_count, num_heads, head_size)
    scaled_v = (-scale_out * token_rates[:, :, None] * value_heads.astype(jnp.float32)).astype(
        jnp.bfloat16
    )
    gathered = lax.all_gather(fast_weights, "seq", axis=0, tiled=True)
    out_sum, hidden_k, grad_first, grad_third = hidden_block(
        query_heads, key_heads, scaled_v, gathered
    )
    applied = out_sum.astype(jnp.bfloat16).reshape(row_count, num_heads * head_size)
    terms = (
        scale_in
        * jnp.einsum("thj,thd->jhd", grad_first, key_heads, preferred_element_type=jnp.float32),
        scale_in
        * jnp.einsum("thj,thd->jhd", grad_third, key_heads, preferred_element_type=jnp.float32),
        jnp.einsum("thj,thd->jhd", hidden_k, scaled_v, preferred_element_type=jnp.float32),
    )
    sums = [
        jnp.sum(
            lax.all_to_all(term[:, None], "seq", split_axis=0, concat_axis=1, tiled=True), axis=1
        )
        for term in terms
    ]
    gradient = jnp.stack(sums, axis=1)
    partial_gram = jnp.einsum("jmhd,jmhe->mhde", gradient, gradient, precision=exact)
    gram_matrix = lax.psum(partial_gram, "seq")
    poly_factor = newton_factor(gram_matrix)
    update = jnp.einsum("mhde,jmhe->jmhd", poly_factor, gradient, precision=exact)
    renewed = (fast_weights.astype(jnp.float32) - math.sqrt(HID) * update).astype(jnp.bfloat16)
    return (applied, renewed)


def body(size, queries, key_vectors, value_vectors, token_rates, fast_weights):
    planes = size // PLANE
    if size == PLANE * planes and planes > 1 and fast_weights.shape[2] % planes == 0:
        return plane_body(
            queries, key_vectors, value_vectors, token_rates, fast_weights, planes
        )
    return gather_body(queries, key_vectors, value_vectors, token_rates, fast_weights)


def solution(mesh):
    in_specs = (
        P(("groups", "seq"), None),
        P(("groups", "seq"), None),
        P(("groups", "seq"), None),
        P(("groups", "seq"), None),
        P(("groups", "seq"), None, None, None),
    )
    out_specs = (P(("groups", "seq"), None), P(("groups", "seq"), None, None, None))
    return jax.shard_map(
        functools.partial(body, mesh.shape["seq"]),
        mesh=mesh,
        in_specs=in_specs,
        out_specs=out_specs,
        check_vma=False,
    )
```

```python
import functools
import math

import jax
import jax.numpy as jnp
from jax import lax
from jax.experimental import pallas as pl
from jax.experimental.pallas import tpu as pltpu
from jax.sharding import PartitionSpec as P

HID = 512
NS_STEPS = 2
PLACES = 4

coef_a = 3.4445
coef_b = -4.775
coef_c = 2.0315

VMEM = pltpu.VMEM
SMEM = pltpu.SMEM
NT = (((1,), (1,)), ((), ()))
NN = (((1,), (0,)), ((), ()))
TN = (((0,), (0,)), ((), ()))


def dot(a, b, dims, precision=None):
    return lax.dot_general(a, b, dims, precision=precision, preferred_element_type=jnp.float32)


def split_kernel(where_ref, q_ref, k_ref, v_ref, rate_ref, *refs):
    outs, scaled = refs[:-1], refs[-1]
    spot = where_ref[0]
    width = outs[0].shape[2]
    num_heads = rate_ref.shape[1]
    head_size = k_ref.shape[1] // num_heads
    rates = (-1.0 / math.sqrt(HID)) * rate_ref[...]
    for head in range(num_heads):
        at = slice(head * head_size, (head + 1) * head_size)
        scaled[:, at] = (rates[:, head : head + 1] * v_ref[:, at].astype(jnp.float32)).astype(
            jnp.bfloat16
        )
    for rel, out_ref in enumerate(outs):
        at = pl.multiple_of((spot ^ rel) * width, width)
        out_ref[0] = k_ref[:, pl.ds(at, width)]
        out_ref[1] = scaled[:, pl.ds(at, width)]
        out_ref[2] = q_ref[:, pl.ds(at, width)]


def join_kernel(where_ref, *refs):
    ins, (out_ref, done_ref) = refs[:-2], refs[-2:]
    spot = where_ref[0]
    width = ins[0].shape[1]
    for rel, in_ref in enumerate(ins):
        at = pl.multiple_of((spot ^ rel) * width, width)
        out_ref[:, pl.ds(at, width)] = in_ref[...]
    done_ref[...] = jnp.zeros_like(done_ref)


def weight_rows(w_refs, rel, matrix):
    pieces = w_refs[2 * rel : 2 * rel + 2]
    return jnp.concatenate(
        [w[at, 0, matrix] for w in pieces for at in range(w.shape[0])], axis=0
    )


def key_kernel(squares, begin, first_slot, slots, last, where_ref, *refs):
    pairs, w_refs, carried = refs[:squares], refs[squares : squares + 8], refs[squares + 8]
    keep_ref, near_ref = refs[squares + 9 : squares + 11]
    far_refs = refs[squares + 11 : squares + 11 + slots]
    carry_ref, terms = refs[-2:]
    spot, place = where_ref[0], where_ref[1]
    _, hid, head_size = terms.shape
    rows = hid // (PLACES * squares)
    step = pl.program_id(0)
    scale_in = 1.0 / math.sqrt(head_size)

    def put(number, value):
        rel = (number % PLACES) ^ place
        slot = number // PLACES - first_slot

        @pl.when((rel % 2 == 0) & (slot < slots))
        def _():
            keep_ref[rel // 2, slot] = value

        @pl.when((rel == 1) & (slot < slots))
        def _():
            near_ref[slot] = value.astype(near_ref.dtype)

        for one in range(slots):

            @pl.when((rel == 3) & (slot == one))
            def _():
                far_refs[one][...] = value.astype(far_refs[one].dtype)

        if not last:

            @pl.when(slot >= slots)
            def _():
                carry_ref[number - PLACES * (first_slot + slots)] = value

    @pl.when(step == 0)
    def _():
        if first_slot:
            for number in range(PLACES * first_slot, 3 * begin):
                put(number, carried[number - PLACES * first_slot])
        if last:
            for number in range(3 * last, PLACES * (first_slot + slots)):
                put(number, jnp.zeros((hid, head_size), jnp.float32))

    keys = jnp.concatenate([pair[0] for pair in pairs], axis=0)
    scaled = jnp.concatenate([pair[1] for pair in pairs], axis=0)
    for rel in range(PLACES):
        raw_first = dot(weight_rows(w_refs, rel, 0), keys, NT)
        raw_third = dot(weight_rows(w_refs, rel, 1), keys, NT)
        back = dot(weight_rows(w_refs, rel, 2), scaled, NT)
        first = raw_first * scale_in
        sig = 0.5 * jnp.tanh(0.5 * first) + 0.5
        act = first * sig
        hidden = (act * raw_third).astype(jnp.bfloat16)
        grad_third = (back * act).astype(jnp.bfloat16)
        slope = sig + act * (1.0 - sig)
        grad_first = (back * raw_third * slope).astype(jnp.bfloat16)
        values = (
            dot(grad_first, keys, NN) * (scale_in * scale_in),
            dot(grad_third, keys, NN) * scale_in,
            dot(hidden, scaled, NN) * scale_in,
        )
        for apart in range(squares):
            to = pl.multiple_of(((place ^ rel) * squares + (spot ^ apart)) * rows, rows)
            for matrix in range(3):
                terms[matrix, pl.ds(to, rows), :] = values[matrix][apart * rows : (apart + 1) * rows]
    for matrix in range(3):
        put(3 * (begin + step) + matrix, terms[matrix])


def query_kernel(squares, *refs):
    ins, w_refs, outs = refs[:squares], refs[squares : squares + 8], refs[-squares:]
    scale_in = 1.0 / math.sqrt(ins[0].shape[2])
    scale_out = 1.0 / math.sqrt(HID)
    first_map, third_map, second = (
        jnp.concatenate([weight_rows(w_refs, rel, matrix) for rel in range(PLACES)], axis=0)
        for matrix in range(3)
    )
    for q_ref, out_ref in zip(ins, outs):
        queries = q_ref[0]
        first = dot(queries, first_map, NT) * scale_in
        third = dot(queries, third_map, NT) * scale_in
        sig = 0.5 * jnp.tanh(0.5 * first) + 0.5
        hidden = (first * sig * third).astype(jnp.bfloat16)
        out_ref[...] = (dot(hidden, second, NN) * scale_out).astype(out_ref.dtype)


def renew_kernel(squares, first_slot, where_ref, mine_ref, near_ref, far_ref, *refs):
    w_refs, (out_ref, updates) = refs[:8], refs[-2:]
    spot, place = where_ref[0], where_ref[1]
    slots, hid, head_size = far_ref.shape
    heads = w_refs[0].shape[1]
    rows = out_ref.shape[2]
    exact = lax.Precision.HIGHEST
    eye = (
        lax.broadcasted_iota(jnp.int32, (head_size, head_size), 0)
        == lax.broadcasted_iota(jnp.int32, (head_size, head_size), 1)
    ).astype(jnp.float32)
    grads = [
        mine_ref[0, slot]
        + near_ref[slot].astype(jnp.float32)
        + far_ref[slot].astype(jnp.float32)
        for slot in range(slots)
    ]
    grams = [dot(grad, grad, TN, exact) for grad in grads]
    factors = [eye * (1.0 / (jnp.sqrt(jnp.sum(gram * eye)) + 1e-07)) for gram in grams]
    for _ in range(NS_STEPS):
        inner = [dot(gram, factor, NN, exact) for gram, factor in zip(grams, factors)]
        square = [dot(factor, term, NN, exact) for factor, term in zip(factors, inner)]
        mixed = [coef_b * term + coef_c * dot(term, term, NN, exact) for term in square]
        factors = [
            coef_a * factor + dot(term, factor, NN, exact) for term, factor in zip(mixed, factors)
        ]
    for slot in range(slots):
        updates[slot] = math.sqrt(HID) * dot(grads[slot], factors[slot], NT, exact)
    for slot in range(slots):
        number = jnp.minimum(PLACES * (first_slot + slot) + place, 3 * heads - 1)
        head, matrix = number // 3, number % 3
        for rel in range(PLACES):
            owner = place ^ rel
            for apart in range(squares):
                w = w_refs[2 * rel + apart // (squares // 2)]
                at = pl.multiple_of((owner * squares + (spot ^ apart)) * rows, rows)
                to = (owner // 2 * squares + (spot ^ apart)) * 2 + owner % 2
                old = w[apart % (squares // 2), head, matrix].astype(jnp.float32)
                out_ref[to, slot] = (old - updates[slot, pl.ds(at, rows), :]).astype(out_ref.dtype)


def square_body(queries, key_vectors, value_vectors, token_rates, fast_weights, squares):
    row_count = queries.shape[0]
    own_rows, _, num_heads, head_size = fast_weights.shape
    heads = num_heads // squares
    width = heads * head_size
    size = squares * PLACES
    half = size // 2
    hid = size * own_rows
    cut = squares // 2
    position = lax.axis_index("seq").astype(jnp.int32)
    spot = position % half // 2
    where = jnp.stack([spot, 2 * (position // half) + position % 2])
    params = pltpu.CompilerParams(vmem_limit_bytes=40 * 2**20)
    smem = pl.BlockSpec(memory_space=SMEM)
    vmem = pl.BlockSpec(memory_space=VMEM)

    def cost(mega_flops):
        return pl.CostEstimate(
            flops=mega_flops * 10**6, bytes_accessed=4 * 10**6, transcendentals=0
        )

    def swap(array, step):
        return lax.ppermute(array, "seq", [(at, at ^ step) for at in range(size)])

    def across(pieces):
        return [pieces[0]] + [swap(pieces[rel], 2 * rel) for rel in range(1, squares)]

    def bf16(*shape):
        return jax.ShapeDtypeStruct(shape, jnp.bfloat16)

    token = jax.ShapeDtypeStruct((8, 128), jnp.float32)

    moved = across(
        pl.pallas_call(
            split_kernel,
            in_specs=[smem] + [vmem] * 4,
            out_specs=[vmem] * squares,
            out_shape=[bf16(3, row_count, width)] * squares,
            scratch_shapes=[VMEM((row_count, num_heads * head_size), jnp.bfloat16)],
            compiler_params=params,
            cost_estimate=cost(10),
            name="split",
        )(where, queries, key_vectors, value_vectors, token_rates)
    )

    by_spot = fast_weights.reshape(own_rows, 3, squares, heads, head_size).transpose(2, 3, 1, 0, 4)
    pieces = across(
        [
            lax.dynamic_index_in_dim(by_spot, spot ^ rel, 0, keepdims=False)
            for rel in range(squares)
        ]
    )
    own = [jnp.stack(pieces[:cut]), jnp.stack(pieces[cut:])]
    other = [swap(w, half) for w in own]
    weights = [own, [swap(w, 1) for w in own], other, [swap(w, 1) for w in other]]
    weights = [w for pair in weights for w in pair]

    def weight_spec(begin=0):
        return pl.BlockSpec((cut, 1, 3, own_rows, head_size), lambda h: (0, h + begin, 0, 0, 0))

    def key_side(begin, end, first_slot, slots, carry_count, carried):
        keep_shape = (2, slots, hid, head_size)
        carry_shape = (max(carry_count, 1), hid, head_size)

        def whole(shape):
            return pl.BlockSpec(shape, lambda h: (0,) * len(shape))

        return pl.pallas_call(
            functools.partial(
                key_kernel, squares, begin, first_slot, slots, heads if end == heads else 0
            ),
            grid=(end - begin,),
            in_specs=[
                smem,
                *[pl.BlockSpec((2, row_count, head_size), lambda h: (0, 0, h + begin))] * squares,
                *[weight_spec(begin)] * 8,
                whole(carried.shape) if begin else smem,
            ],
            out_specs=[whole(keep_shape), whole(keep_shape[1:])]
            + [whole(keep_shape[2:])] * slots
            + [whole(carry_shape)],
            out_shape=[jax.ShapeDtypeStruct(keep_shape, jnp.float32), bf16(*keep_shape[1:])]
            + [bf16(*keep_shape[2:])] * slots
            + [jax.ShapeDtypeStruct(carry_shape, jnp.float32)],
            scratch_shapes=[VMEM((3, hid, head_size), jnp.float32)],
            compiler_params=params,
            cost_estimate=cost(1000),
            name="key_side",
        )(where, *moved, *weights, carried)

    def add_up(keep, near, *far):
        got = jnp.stack([swap(one, 1) for one in far])
        other = (keep[1] + got.astype(jnp.float32)).astype(jnp.bfloat16)
        return keep, swap(near, 1), swap(other, half)

    middle = -(-heads // 2)
    slots_all = -(-3 * heads // PLACES)
    slots_one = 3 * middle // PLACES
    *sums_one, carry = key_side(0, middle, 0, slots_one, 3 * middle - PLACES * slots_one, where)
    sums_one = add_up(*sums_one)
    *sums_two, _ = key_side(middle, heads, slots_one, slots_all - slots_one, 0, carry)
    sums_two = add_up(*sums_two)

    columns = pl.BlockSpec((row_count, head_size), lambda h: (0, h))
    parts = pl.pallas_call(
        functools.partial(query_kernel, squares),
        grid=(heads,),
        in_specs=[pl.BlockSpec((1, row_count, head_size), lambda h: (2, 0, h))] * squares
        + [weight_spec()] * 8,
        out_specs=[columns] * squares,
        out_shape=[bf16(row_count, width)] * squares,
        compiler_params=params,
        cost_estimate=cost(1000),
        name="query_side",
    )(*moved, *weights)
    applied, joined = pl.pallas_call(
        join_kernel,
        in_specs=[smem] + [vmem] * squares,
        out_specs=[vmem] * 2,
        out_shape=[bf16(row_count, num_heads * head_size), token],
        compiler_params=params,
        cost_estimate=cost(10),
        name="join",
    )(where, *across(parts))

    def renew(keep, near, far, first_slot, before):
        slots = far.shape[0]
        return pl.pallas_call(
            functools.partial(renew_kernel, squares, first_slot),
            in_specs=[smem] + [vmem] * (11 + len(before)),
            out_specs=vmem,
            out_shape=bf16(size, slots, own_rows, head_size),
            scratch_shapes=[VMEM((slots, hid, head_size), jnp.float32)],
            compiler_params=params,
            cost_estimate=cost(1000),
            name="renew",
        )(where, keep, near, far, *weights, *before)

    renewed = jnp.concatenate(
        [renew(*sums_one, 0, ()), renew(*sums_two, slots_one, (joined,))], axis=1
    )
    back = lax.all_to_all(renewed, "seq", 0, 0, tiled=True)
    back = back.reshape(2, squares, 2, slots_all, own_rows, head_size).transpose(1, 3, 0, 2, 4, 5)
    back = back.reshape(squares, PLACES * slots_all, own_rows, head_size)[:, : 3 * heads]
    renewed_out = (
        back.reshape(squares, heads, 3, own_rows, head_size)
        .transpose(3, 2, 0, 1, 4)
        .reshape(own_rows, 3, num_heads, head_size)
    )
    return applied, renewed_out


def newton_factor(gram_matrix):
    exact = lax.Precision.HIGHEST
    head_size = gram_matrix.shape[-1]
    trace_sum = jnp.trace(gram_matrix, axis1=-2, axis2=-1)
    factor = 1.0 / (jnp.sqrt(trace_sum) + 1e-07)
    poly_factor = factor[..., None, None] * jnp.eye(head_size, dtype=jnp.float32)
    for newton_step in range(NS_STEPS):
        inner_term = jnp.matmul(gram_matrix, poly_factor, precision=exact)
        square = jnp.matmul(poly_factor, inner_term, precision=exact)
        mixed_term = coef_b * square + coef_c * jnp.matmul(square, square, precision=exact)
        poly_factor = coef_a * poly_factor + jnp.matmul(mixed_term, poly_factor, precision=exact)
    return poly_factor


def hidden_block(query_heads, key_heads, scaled_v, weight_block):
    head_size = query_heads.shape[2]
    scale_in = 1.0 / math.sqrt(head_size)
    scale_out = 1.0 / math.sqrt(HID)
    query_first = scale_in * jnp.einsum(
        "thd,jhd->thj", query_heads, weight_block[:, 0], preferred_element_type=jnp.float32
    )
    query_third = scale_in * jnp.einsum(
        "thd,jhd->thj", query_heads, weight_block[:, 1], preferred_element_type=jnp.float32
    )
    hidden_q = (query_first * jax.nn.sigmoid(query_first) * query_third).astype(jnp.bfloat16)
    partial_out = scale_out * jnp.einsum(
        "thj,jhd->thd", hidden_q, weight_block[:, 2], preferred_element_type=jnp.float32
    )
    key_first = scale_in * jnp.einsum(
        "thd,jhd->thj", key_heads, weight_block[:, 0], preferred_element_type=jnp.float32
    )
    key_third = scale_in * jnp.einsum(
        "thd,jhd->thj", key_heads, weight_block[:, 1], preferred_element_type=jnp.float32
    )
    sigmoid_k = jax.nn.sigmoid(key_first)
    activated = key_first * sigmoid_k
    hidden_k = (activated * key_third).astype(jnp.bfloat16)
    back_grad = jnp.einsum(
        "thd,jhd->thj", scaled_v, weight_block[:, 2], preferred_element_type=jnp.float32
    )
    grad_third = (back_grad * activated).astype(jnp.bfloat16)
    grad_first = (back_grad * key_third * sigmoid_k * (1.0 + key_first * (1.0 - sigmoid_k))).astype(
        jnp.bfloat16
    )
    return (partial_out, hidden_k, grad_first, grad_third)


def gather_body(queries, key_vectors, value_vectors, token_rates, fast_weights):
    exact = lax.Precision.HIGHEST
    row_count = queries.shape[0]
    num_heads = fast_weights.shape[2]
    head_size = fast_weights.shape[3]
    scale_in = 1.0 / math.sqrt(head_size)
    scale_out = 1.0 / math.sqrt(HID)
    query_heads = queries.reshape(row_count, num_heads, head_size)
    key_heads = key_vectors.reshape(row_count, num_heads, head_size)
    value_heads = value_vectors.reshape(row_count, num_heads, head_size)
    scaled_v = (-scale_out * token_rates[:, :, None] * value_heads.astype(jnp.float32)).astype(
        jnp.bfloat16
    )
    gathered = lax.all_gather(fast_weights, "seq", axis=0, tiled=True)
    out_sum, hidden_k, grad_first, grad_third = hidden_block(
        query_heads, key_heads, scaled_v, gathered
    )
    applied = out_sum.astype(jnp.bfloat16).reshape(row_count, num_heads * head_size)
    terms = (
        scale_in
        * jnp.einsum("thj,thd->jhd", grad_first, key_heads, preferred_element_type=jnp.float32),
        scale_in
        * jnp.einsum("thj,thd->jhd", grad_third, key_heads, preferred_element_type=jnp.float32),
        jnp.einsum("thj,thd->jhd", hidden_k, scaled_v, preferred_element_type=jnp.float32),
    )
    sums = [
        jnp.sum(
            lax.all_to_all(term[:, None], "seq", split_axis=0, concat_axis=1, tiled=True), axis=1
        )
        for term in terms
    ]
    gradient = jnp.stack(sums, axis=1)
    partial_gram = jnp.einsum("jmhd,jmhe->mhde", gradient, gradient, precision=exact)
    gram_matrix = lax.psum(partial_gram, "seq")
    poly_factor = newton_factor(gram_matrix)
    update = jnp.einsum("mhde,jmhe->jmhd", poly_factor, gradient, precision=exact)
    renewed = (fast_weights.astype(jnp.float32) - math.sqrt(HID) * update).astype(jnp.bfloat16)
    return (applied, renewed)


def body(size, queries, key_vectors, value_vectors, token_rates, fast_weights):
    squares = size // PLACES
    if (
        size == PLACES * squares
        and squares > 1
        and squares & (squares - 1) == 0
        and fast_weights.shape[2] % squares == 0
    ):
        return square_body(
            queries, key_vectors, value_vectors, token_rates, fast_weights, squares
        )
    return gather_body(queries, key_vectors, value_vectors, token_rates, fast_weights)


def solution(mesh):
    in_specs = (
        P(("groups", "seq"), None),
        P(("groups", "seq"), None),
        P(("groups", "seq"), None),
        P(("groups", "seq"), None),
        P(("groups", "seq"), None, None, None),
    )
    out_specs = (P(("groups", "seq"), None), P(("groups", "seq"), None, None, None))
    return jax.shard_map(
        functools.partial(body, mesh.shape["seq"]),
        mesh=mesh,
        in_specs=in_specs,
        out_specs=out_specs,
        check_vma=False,
    )
```

```python
import functools
import math

import jax
import jax.numpy as jnp
from jax import lax
from jax.experimental import pallas as pl
from jax.experimental.pallas import tpu as pltpu
from jax.sharding import PartitionSpec as P

HID = 512
NS_STEPS = 2
PLACES = 4

coef_a = 3.4445
coef_b = -4.775
coef_c = 2.0315

VMEM = pltpu.VMEM
SMEM = pltpu.SMEM
NT = (((1,), (1,)), ((), ()))
NN = (((1,), (0,)), ((), ()))
TN = (((0,), (0,)), ((), ()))


def dot(a, b, dims, precision=None):
    return lax.dot_general(a, b, dims, precision=precision, preferred_element_type=jnp.float32)


def split_kernel(where_ref, q_ref, k_ref, v_ref, rate_ref, *refs):
    outs, scaled = refs[:-1], refs[-1]
    spot = where_ref[0]
    width = outs[0].shape[2]
    num_heads = rate_ref.shape[1]
    head_size = k_ref.shape[1] // num_heads
    rates = (-1.0 / math.sqrt(HID)) * rate_ref[...]
    for head in range(num_heads):
        at = slice(head * head_size, (head + 1) * head_size)
        scaled[:, at] = (rates[:, head : head + 1] * v_ref[:, at].astype(jnp.float32)).astype(
            jnp.bfloat16
        )
    for rel, out_ref in enumerate(outs):
        at = pl.multiple_of((spot ^ rel) * width, width)
        out_ref[0] = k_ref[:, pl.ds(at, width)]
        out_ref[1] = scaled[:, pl.ds(at, width)]
        out_ref[2] = q_ref[:, pl.ds(at, width)]


def join_kernel(where_ref, *refs):
    ins, (out_ref, done_ref) = refs[:-2], refs[-2:]
    spot = where_ref[0]
    width = ins[0].shape[1]
    for rel, in_ref in enumerate(ins):
        at = pl.multiple_of((spot ^ rel) * width, width)
        out_ref[:, pl.ds(at, width)] = in_ref[...]
    done_ref[...] = jnp.zeros_like(done_ref)


def weight_rows(w_refs, rel, matrix):
    pieces = w_refs[2 * rel : 2 * rel + 2]
    return jnp.concatenate(
        [w[at, 0, matrix] for w in pieces for at in range(w.shape[0])], axis=0
    )


def key_kernel(squares, heads, where_ref, *refs):
    pairs, w_refs = refs[:squares], refs[squares : squares + 8]
    keep_ref, near_ref, far_ref, terms = refs[squares + 8 :]
    spot, place = where_ref[0], where_ref[1]
    _, hid, head_size = terms.shape
    rows = hid // (PLACES * squares)
    step = pl.program_id(0)
    scale_in = 1.0 / math.sqrt(head_size)

    def put(number, value):
        rel = (number % PLACES) ^ place
        slot = number // PLACES

        @pl.when(rel % 2 == 0)
        def _():
            keep_ref[rel // 2, slot] = value

        @pl.when(rel == 1)
        def _():
            near_ref[slot] = value.astype(near_ref.dtype)

        @pl.when(rel == 3)
        def _():
            far_ref[slot] = value.astype(far_ref.dtype)

    @pl.when(step == 0)
    def _():
        for number in range(3 * heads, PLACES * keep_ref.shape[1]):
            put(number, jnp.zeros((hid, head_size), jnp.float32))

    keys = jnp.concatenate([pair[0] for pair in pairs], axis=0)
    scaled = jnp.concatenate([pair[1] for pair in pairs], axis=0)
    both_maps = jnp.concatenate(
        [weight_rows(w_refs, rel, matrix) for matrix in range(2) for rel in range(PLACES)], axis=0
    )
    second = jnp.concatenate([weight_rows(w_refs, rel, 2) for rel in range(PLACES)], axis=0)
    raw = dot(both_maps, keys, NT)
    raw_third = raw[hid:]
    back = dot(second, scaled, NT)
    half_first = raw[:hid] * (0.5 * scale_in)
    tanh = jnp.tanh(half_first)
    act = half_first + half_first * tanh
    hidden = (act * raw_third).astype(jnp.bfloat16)
    grad_third = (back * act).astype(jnp.bfloat16)
    twice_slope = (1.0 + tanh) + act * (1.0 - tanh)
    grad_first = (back * raw_third * twice_slope).astype(jnp.bfloat16)
    firsts = dot(jnp.concatenate([grad_first, grad_third], axis=0), keys, NN)
    values = (
        firsts[:hid] * (0.5 * scale_in * scale_in),
        firsts[hid:] * scale_in,
        dot(hidden, scaled, NN) * scale_in,
    )
    for rel in range(PLACES):
        for apart in range(squares):
            at = (rel * squares + apart) * rows
            to = pl.multiple_of(((place ^ rel) * squares + (spot ^ apart)) * rows, rows)
            for matrix in range(3):
                terms[matrix, pl.ds(to, rows), :] = values[matrix][at : at + rows]
    for matrix in range(3):
        put(3 * step + matrix, terms[matrix])


def query_kernel(squares, *refs):
    ins, w_refs, outs = refs[:squares], refs[squares : squares + 8], refs[-squares:]
    scale_in = 1.0 / math.sqrt(ins[0].shape[2])
    scale_out = 1.0 / math.sqrt(HID)
    first_map, third_map, second = (
        jnp.concatenate([weight_rows(w_refs, rel, matrix) for rel in range(PLACES)], axis=0)
        for matrix in range(3)
    )
    queries = jnp.concatenate([q_ref[0] for q_ref in ins], axis=0)
    half_first = dot(queries, first_map, NT) * (0.5 * scale_in)
    third = dot(queries, third_map, NT)
    hidden = ((half_first + half_first * jnp.tanh(half_first)) * third).astype(jnp.bfloat16)
    out = (dot(hidden, second, NN) * (scale_in * scale_out)).astype(jnp.bfloat16)
    rows = outs[0].shape[0]
    for rel, out_ref in enumerate(outs):
        out_ref[...] = out[rel * rows : (rel + 1) * rows]


def halves(array):
    high = array.astype(jnp.bfloat16)
    return high, (array - high.astype(jnp.float32)).astype(jnp.bfloat16)


def dot_halves(a, b, dims):
    return dot(a[0], b[0], dims) + (dot(a[0], b[1], dims) + dot(a[1], b[0], dims))


def renew_kernel(squares, where_ref, mine_ref, near_ref, far_ref, *refs):
    w_refs, (out_ref, updates) = refs[:8], refs[-2:]
    spot, place = where_ref[0], where_ref[1]
    slots, hid, head_size = far_ref.shape
    heads = w_refs[0].shape[1]
    rows = out_ref.shape[2]
    eye = (
        lax.broadcasted_iota(jnp.int32, (head_size, head_size), 0)
        == lax.broadcasted_iota(jnp.int32, (head_size, head_size), 1)
    ).astype(jnp.float32)
    grads = [
        mine_ref[0, slot]
        + near_ref[slot].astype(jnp.float32)
        + far_ref[slot].astype(jnp.float32)
        for slot in range(slots)
    ]
    grads = [halves(grad) for grad in grads]
    grams = []
    for high, low in grads:
        cross = dot(high, low, TN)
        grams.append(dot(high, high, TN) + (cross + cross.T))
    scales = [1.0 / (jnp.sqrt(jnp.sum(gram * eye)) + 1e-07) for gram in grams]
    factors = []
    for gram, scale in zip(grams, scales):
        square = (scale * scale) * gram
        parts = halves(square)
        factors.append(
            scale * (coef_a * eye + coef_b * square + coef_c * dot_halves(parts, parts, NN))
        )
    grams = [halves(gram) for gram in grams]
    for _ in range(NS_STEPS - 1):
        parts = [halves(factor) for factor in factors]
        inner = [dot_halves(gram, part, NN) for gram, part in zip(grams, parts)]
        squares_of = [dot_halves(part, halves(term), NN) for part, term in zip(parts, inner)]
        mixed = []
        for square in squares_of:
            term = halves(square)
            mixed.append(coef_b * square + coef_c * dot_halves(term, term, NN))
        factors = [
            coef_a * factor + dot_halves(halves(term), part, NN)
            for term, factor, part in zip(mixed, factors, parts)
        ]
    for slot in range(slots):
        updates[slot] = math.sqrt(HID) * dot_halves(grads[slot], halves(factors[slot]), NT)
    for slot in range(slots):
        number = jnp.minimum(PLACES * slot + place, 3 * heads - 1)
        head, matrix = number // 3, number % 3
        for rel in range(PLACES):
            owner = place ^ rel
            for apart in range(squares):
                w = w_refs[2 * rel + apart // (squares // 2)]
                at = pl.multiple_of((owner * squares + (spot ^ apart)) * rows, rows)
                to = (owner // 2 * squares + (spot ^ apart)) * 2 + owner % 2
                old = w[apart % (squares // 2), head, matrix].astype(jnp.float32)
                out_ref[to, slot] = (old - updates[slot, pl.ds(at, rows), :]).astype(out_ref.dtype)


def square_body(queries, key_vectors, value_vectors, token_rates, fast_weights, squares):
    row_count = queries.shape[0]
    own_rows, _, num_heads, head_size = fast_weights.shape
    heads = num_heads // squares
    width = heads * head_size
    size = squares * PLACES
    half = size // 2
    hid = size * own_rows
    cut = squares // 2
    position = lax.axis_index("seq").astype(jnp.int32)
    spot = position % half // 2
    where = jnp.stack([spot, 2 * (position // half) + position % 2])
    params = pltpu.CompilerParams(vmem_limit_bytes=40 * 2**20)
    smem = pl.BlockSpec(memory_space=SMEM)
    vmem = pl.BlockSpec(memory_space=VMEM)

    def cost(mega_flops):
        return pl.CostEstimate(
            flops=mega_flops * 10**6, bytes_accessed=4 * 10**6, transcendentals=0
        )

    def swap(array, step):
        return lax.ppermute(array, "seq", [(at, at ^ step) for at in range(size)])

    def across(pieces):
        return [pieces[0]] + [swap(pieces[rel], 2 * rel) for rel in range(1, squares)]

    def bf16(*shape):
        return jax.ShapeDtypeStruct(shape, jnp.bfloat16)

    token = jax.ShapeDtypeStruct((8, 128), jnp.float32)

    moved = across(
        pl.pallas_call(
            split_kernel,
            in_specs=[smem] + [vmem] * 4,
            out_specs=[vmem] * squares,
            out_shape=[bf16(3, row_count, width)] * squares,
            scratch_shapes=[VMEM((row_count, num_heads * head_size), jnp.bfloat16)],
            compiler_params=params,
            cost_estimate=cost(10),
            name="split",
        )(where, queries, key_vectors, value_vectors, token_rates)
    )

    by_spot = fast_weights.reshape(own_rows, 3, squares, heads, head_size).transpose(2, 3, 1, 0, 4)
    pieces = across(
        [
            lax.dynamic_index_in_dim(by_spot, spot ^ rel, 0, keepdims=False)
            for rel in range(squares)
        ]
    )
    own = [jnp.stack(pieces[:cut]), jnp.stack(pieces[cut:])]
    other = [swap(w, half) for w in own]
    weights = [own, [swap(w, 1) for w in own], other, [swap(w, 1) for w in other]]
    weights = [w for pair in weights for w in pair]

    weight_spec = pl.BlockSpec((cut, 1, 3, own_rows, head_size), lambda h: (0, h, 0, 0, 0))

    slots = -(-3 * heads // PLACES)
    sums_shape = (slots, hid, head_size)
    keep, near, far = pl.pallas_call(
        functools.partial(key_kernel, squares, heads),
        grid=(heads,),
        in_specs=[smem]
        + [pl.BlockSpec((2, row_count, head_size), lambda h: (0, 0, h))] * squares
        + [weight_spec] * 8,
        out_specs=[pl.BlockSpec((2, *sums_shape), lambda h: (0, 0, 0, 0))]
        + [pl.BlockSpec(sums_shape, lambda h: (0, 0, 0))] * 2,
        out_shape=[
            jax.ShapeDtypeStruct((2, *sums_shape), jnp.float32),
            bf16(*sums_shape),
            bf16(*sums_shape),
        ],
        scratch_shapes=[VMEM((3, hid, head_size), jnp.float32)],
        compiler_params=params,
        cost_estimate=cost(2000),
        name="key_side",
    )(where, *moved, *weights)

    near = swap(near, 1)
    far = swap((keep[1] + swap(far, 1).astype(jnp.float32)).astype(jnp.bfloat16), half)

    columns = pl.BlockSpec((row_count, head_size), lambda h: (0, h))
    parts = pl.pallas_call(
        functools.partial(query_kernel, squares),
        grid=(heads,),
        in_specs=[pl.BlockSpec((1, row_count, head_size), lambda h: (2, 0, h))] * squares
        + [weight_spec] * 8,
        out_specs=[columns] * squares,
        out_shape=[bf16(row_count, width)] * squares,
        compiler_params=params,
        cost_estimate=cost(1000),
        name="query_side",
    )(*moved, *weights)
    applied, joined = pl.pallas_call(
        join_kernel,
        in_specs=[smem] + [vmem] * squares,
        out_specs=[vmem] * 2,
        out_shape=[bf16(row_count, num_heads * head_size), token],
        compiler_params=params,
        cost_estimate=cost(10),
        name="join",
    )(where, *across(parts))

    renewed = pl.pallas_call(
        functools.partial(renew_kernel, squares),
        in_specs=[smem] + [vmem] * 12,
        out_specs=vmem,
        out_shape=bf16(size, slots, own_rows, head_size),
        scratch_shapes=[VMEM(sums_shape, jnp.float32)],
        compiler_params=params,
        cost_estimate=cost(2000),
        name="renew",
    )(where, keep, near, far, *weights, joined)
    back = lax.all_to_all(renewed, "seq", 0, 0, tiled=True)
    back = back.reshape(2, squares, 2, slots, own_rows, head_size).transpose(1, 3, 0, 2, 4, 5)
    back = back.reshape(squares, PLACES * slots, own_rows, head_size)[:, : 3 * heads]
    renewed_out = (
        back.reshape(squares, heads, 3, own_rows, head_size)
        .transpose(3, 2, 0, 1, 4)
        .reshape(own_rows, 3, num_heads, head_size)
    )
    return applied, renewed_out


def newton_factor(gram_matrix):
    exact = lax.Precision.HIGHEST
    head_size = gram_matrix.shape[-1]
    trace_sum = jnp.trace(gram_matrix, axis1=-2, axis2=-1)
    factor = 1.0 / (jnp.sqrt(trace_sum) + 1e-07)
    poly_factor = factor[..., None, None] * jnp.eye(head_size, dtype=jnp.float32)
    for newton_step in range(NS_STEPS):
        inner_term = jnp.matmul(gram_matrix, poly_factor, precision=exact)
        square = jnp.matmul(poly_factor, inner_term, precision=exact)
        mixed_term = coef_b * square + coef_c * jnp.matmul(square, square, precision=exact)
        poly_factor = coef_a * poly_factor + jnp.matmul(mixed_term, poly_factor, precision=exact)
    return poly_factor


def hidden_block(query_heads, key_heads, scaled_v, weight_block):
    head_size = query_heads.shape[2]
    scale_in = 1.0 / math.sqrt(head_size)
    scale_out = 1.0 / math.sqrt(HID)
    query_first = scale_in * jnp.einsum(
        "thd,jhd->thj", query_heads, weight_block[:, 0], preferred_element_type=jnp.float32
    )
    query_third = scale_in * jnp.einsum(
        "thd,jhd->thj", query_heads, weight_block[:, 1], preferred_element_type=jnp.float32
    )
    hidden_q = (query_first * jax.nn.sigmoid(query_first) * query_third).astype(jnp.bfloat16)
    partial_out = scale_out * jnp.einsum(
        "thj,jhd->thd", hidden_q, weight_block[:, 2], preferred_element_type=jnp.float32
    )
    key_first = scale_in * jnp.einsum(
        "thd,jhd->thj", key_heads, weight_block[:, 0], preferred_element_type=jnp.float32
    )
    key_third = scale_in * jnp.einsum(
        "thd,jhd->thj", key_heads, weight_block[:, 1], preferred_element_type=jnp.float32
    )
    sigmoid_k = jax.nn.sigmoid(key_first)
    activated = key_first * sigmoid_k
    hidden_k = (activated * key_third).astype(jnp.bfloat16)
    back_grad = jnp.einsum(
        "thd,jhd->thj", scaled_v, weight_block[:, 2], preferred_element_type=jnp.float32
    )
    grad_third = (back_grad * activated).astype(jnp.bfloat16)
    grad_first = (back_grad * key_third * sigmoid_k * (1.0 + key_first * (1.0 - sigmoid_k))).astype(
        jnp.bfloat16
    )
    return (partial_out, hidden_k, grad_first, grad_third)


def gather_body(queries, key_vectors, value_vectors, token_rates, fast_weights):
    exact = lax.Precision.HIGHEST
    row_count = queries.shape[0]
    num_heads = fast_weights.shape[2]
    head_size = fast_weights.shape[3]
    scale_in = 1.0 / math.sqrt(head_size)
    scale_out = 1.0 / math.sqrt(HID)
    query_heads = queries.reshape(row_count, num_heads, head_size)
    key_heads = key_vectors.reshape(row_count, num_heads, head_size)
    value_heads = value_vectors.reshape(row_count, num_heads, head_size)
    scaled_v = (-scale_out * token_rates[:, :, None] * value_heads.astype(jnp.float32)).astype(
        jnp.bfloat16
    )
    gathered = lax.all_gather(fast_weights, "seq", axis=0, tiled=True)
    out_sum, hidden_k, grad_first, grad_third = hidden_block(
        query_heads, key_heads, scaled_v, gathered
    )
    applied = out_sum.astype(jnp.bfloat16).reshape(row_count, num_heads * head_size)
    terms = (
        scale_in
        * jnp.einsum("thj,thd->jhd", grad_first, key_heads, preferred_element_type=jnp.float32),
        scale_in
        * jnp.einsum("thj,thd->jhd", grad_third, key_heads, preferred_element_type=jnp.float32),
        jnp.einsum("thj,thd->jhd", hidden_k, scaled_v, preferred_element_type=jnp.float32),
    )
    sums = [
        jnp.sum(
            lax.all_to_all(term[:, None], "seq", split_axis=0, concat_axis=1, tiled=True), axis=1
        )
        for term in terms
    ]
    gradient = jnp.stack(sums, axis=1)
    partial_gram = jnp.einsum("jmhd,jmhe->mhde", gradient, gradient, precision=exact)
    gram_matrix = lax.psum(partial_gram, "seq")
    poly_factor = newton_factor(gram_matrix)
    update = jnp.einsum("mhde,jmhe->jmhd", poly_factor, gradient, precision=exact)
    renewed = (fast_weights.astype(jnp.float32) - math.sqrt(HID) * update).astype(jnp.bfloat16)
    return (applied, renewed)


def body(size, queries, key_vectors, value_vectors, token_rates, fast_weights):
    squares = size // PLACES
    if (
        size == PLACES * squares
        and squares > 1
        and squares & (squares - 1) == 0
        and fast_weights.shape[2] % squares == 0
    ):
        return square_body(
            queries, key_vectors, value_vectors, token_rates, fast_weights, squares
        )
    return gather_body(queries, key_vectors, value_vectors, token_rates, fast_weights)


def solution(mesh):
    in_specs = (
        P(("groups", "seq"), None),
        P(("groups", "seq"), None),
        P(("groups", "seq"), None),
        P(("groups", "seq"), None),
        P(("groups", "seq"), None, None, None),
    )
    out_specs = (P(("groups", "seq"), None), P(("groups", "seq"), None, None, None))
    return jax.shard_map(
        functools.partial(body, mesh.shape["seq"]),
        mesh=mesh,
        in_specs=in_specs,
        out_specs=out_specs,
        check_vma=False,
    )
```

```python
import functools
import math

import jax
import jax.numpy as jnp
from jax import lax
from jax.experimental import pallas as pl
from jax.experimental.pallas import tpu as pltpu
from jax.sharding import PartitionSpec as P

HID = 512
NS_STEPS = 2
PLACES = 4

coef_a = 3.4445
coef_b = -4.775
coef_c = 2.0315

VMEM = pltpu.VMEM
SMEM = pltpu.SMEM
NT = (((1,), (1,)), ((), ()))
NN = (((1,), (0,)), ((), ()))
TN = (((0,), (0,)), ((), ()))


def dot(a, b, dims, precision=None):
    return lax.dot_general(a, b, dims, precision=precision, preferred_element_type=jnp.float32)


def split_kernel(where_ref, q_ref, k_ref, v_ref, rate_ref, *refs):
    outs, scaled = refs[:-1], refs[-1]
    spot = where_ref[0]
    width = outs[0].shape[2]
    num_heads = rate_ref.shape[1]
    head_size = k_ref.shape[1] // num_heads
    rates = (-1.0 / math.sqrt(HID)) * rate_ref[...]
    for head in range(num_heads):
        at = slice(head * head_size, (head + 1) * head_size)
        scaled[:, at] = (rates[:, head : head + 1] * v_ref[:, at].astype(jnp.float32)).astype(
            jnp.bfloat16
        )
    for rel, out_ref in enumerate(outs):
        at = pl.multiple_of((spot ^ rel) * width, width)
        out_ref[0] = k_ref[:, pl.ds(at, width)]
        out_ref[1] = scaled[:, pl.ds(at, width)]
        out_ref[2] = q_ref[:, pl.ds(at, width)]


def join_kernel(where_ref, *refs):
    ins, out_ref = refs[:-1], refs[-1]
    spot = where_ref[0]
    width = ins[0].shape[1]
    for rel, in_ref in enumerate(ins):
        at = pl.multiple_of((spot ^ rel) * width, width)
        out_ref[:, pl.ds(at, width)] = in_ref[...]


def weight_rows(w_refs, rel, matrix):
    pieces = w_refs[2 * rel : 2 * rel + 2]
    return jnp.concatenate(
        [w[at, 0, matrix] for w in pieces for at in range(w.shape[0])], axis=0
    )


def key_kernel(squares, heads, where_ref, *refs):
    pairs, w_refs = refs[:squares], refs[squares : squares + 8]
    keep_ref, near_ref, far_ref, terms = refs[squares + 8 :]
    spot, place = where_ref[0], where_ref[1]
    _, hid, head_size = terms.shape
    rows = hid // (PLACES * squares)
    step = pl.program_id(0)
    scale_in = 1.0 / math.sqrt(head_size)

    def put(number, value):
        rel = (number % PLACES) ^ place
        slot = number // PLACES

        @pl.when(rel % 2 == 0)
        def _():
            keep_ref[rel // 2, slot] = value

        @pl.when(rel == 1)
        def _():
            near_ref[slot] = value.astype(near_ref.dtype)

        @pl.when(rel == 3)
        def _():
            far_ref[slot] = value.astype(far_ref.dtype)

    @pl.when(step == 0)
    def _():
        for number in range(3 * heads, PLACES * keep_ref.shape[1]):
            put(number, jnp.zeros((hid, head_size), jnp.float32))

    keys = jnp.concatenate([pair[0] for pair in pairs], axis=0)
    scaled = jnp.concatenate([pair[1] for pair in pairs], axis=0)
    both_maps = jnp.concatenate(
        [weight_rows(w_refs, rel, matrix) for matrix in range(2) for rel in range(PLACES)], axis=0
    )
    second = jnp.concatenate([weight_rows(w_refs, rel, 2) for rel in range(PLACES)], axis=0)
    raw = dot(both_maps, keys, NT)
    third = raw[hid:] * scale_in
    back = dot(second, scaled, NT)
    half_first = raw[:hid] * (0.5 * scale_in)
    tanh = jnp.tanh(half_first)
    act = half_first + half_first * tanh
    hidden = (act * third).astype(jnp.bfloat16)
    grad_third = (back * act).astype(jnp.bfloat16)
    twice_slope = (1.0 + tanh) + act * (1.0 - tanh)
    grad_first = (back * third * twice_slope).astype(jnp.bfloat16)
    firsts = dot(jnp.concatenate([grad_first, grad_third], axis=0), keys, NN)
    values = (
        firsts[:hid] * (0.5 * scale_in),
        firsts[hid:] * scale_in,
        dot(hidden, scaled, NN),
    )
    for rel in range(PLACES):
        for apart in range(squares):
            at = (rel * squares + apart) * rows
            to = pl.multiple_of(((place ^ rel) * squares + (spot ^ apart)) * rows, rows)
            for matrix in range(3):
                terms[matrix, pl.ds(to, rows), :] = values[matrix][at : at + rows]
    for matrix in range(3):
        put(3 * step + matrix, terms[matrix])


def query_kernel(squares, *refs):
    ins, w_refs, outs = refs[:squares], refs[squares : squares + 8], refs[-squares:]
    scale_in = 1.0 / math.sqrt(ins[0].shape[2])
    scale_out = 1.0 / math.sqrt(HID)
    first_map, third_map, second = (
        jnp.concatenate([weight_rows(w_refs, rel, matrix) for rel in range(PLACES)], axis=0)
        for matrix in range(3)
    )
    queries = jnp.concatenate([q_ref[0] for q_ref in ins], axis=0)
    half_first = dot(queries, first_map, NT) * (0.5 * scale_in)
    third = dot(queries, third_map, NT) * scale_in
    hidden = ((half_first + half_first * jnp.tanh(half_first)) * third).astype(jnp.bfloat16)
    out = (dot(hidden, second, NN) * scale_out).astype(jnp.bfloat16)
    rows = outs[0].shape[0]
    for rel, out_ref in enumerate(outs):
        out_ref[...] = out[rel * rows : (rel + 1) * rows]


def halves(array):
    high = array.astype(jnp.bfloat16)
    return high, (array - high.astype(jnp.float32)).astype(jnp.bfloat16)


def dot_halves(a, b, dims):
    return dot(a[0], b[0], dims) + (dot(a[0], b[1], dims) + dot(a[1], b[0], dims))


def renew_kernel(squares, where_ref, mine_ref, near_ref, far_ref, *refs):
    w_refs, (out_ref, updates) = refs[:8], refs[-2:]
    spot, place = where_ref[0], where_ref[1]
    slots, hid, head_size = far_ref.shape
    heads = w_refs[0].shape[1]
    rows = out_ref.shape[2]
    eye = (
        lax.broadcasted_iota(jnp.int32, (head_size, head_size), 0)
        == lax.broadcasted_iota(jnp.int32, (head_size, head_size), 1)
    ).astype(jnp.float32)
    grads = [
        mine_ref[0, slot]
        + near_ref[slot].astype(jnp.float32)
        + far_ref[slot].astype(jnp.float32)
        for slot in range(slots)
    ]
    grads = [halves(grad) for grad in grads]
    grams = []
    for high, low in grads:
        cross = dot(high, low, TN)
        grams.append(dot(high, high, TN) + (cross + cross.T))
    scales = [1.0 / (jnp.sqrt(jnp.sum(gram * eye)) + 1e-07) for gram in grams]
    factors = []
    for gram, scale in zip(grams, scales):
        square = (scale * scale) * gram
        parts = halves(square)
        factors.append(
            scale * (coef_a * eye + coef_b * square + coef_c * dot_halves(parts, parts, NN))
        )
    grams = [halves(gram) for gram in grams]
    for _ in range(NS_STEPS - 1):
        parts = [halves(factor) for factor in factors]
        inner = [dot_halves(gram, part, NN) for gram, part in zip(grams, parts)]
        squares_of = [dot_halves(part, halves(term), NN) for part, term in zip(parts, inner)]
        mixed = []
        for square in squares_of:
            term = halves(square)
            mixed.append(coef_b * square + coef_c * dot_halves(term, term, NN))
        factors = [
            coef_a * factor + dot_halves(halves(term), part, NN)
            for term, factor, part in zip(mixed, factors, parts)
        ]
    for slot in range(slots):
        updates[slot] = math.sqrt(HID) * dot_halves(grads[slot], halves(factors[slot]), NT)
    for slot in range(slots):
        number = jnp.minimum(PLACES * slot + place, 3 * heads - 1)
        head, matrix = number // 3, number % 3
        for rel in range(PLACES):
            owner = place ^ rel
            for apart in range(squares):
                w = w_refs[2 * rel + apart // (squares // 2)]
                at = pl.multiple_of((owner * squares + (spot ^ apart)) * rows, rows)
                to = (owner // 2 * squares + (spot ^ apart)) * 2 + owner % 2
                old = w[apart % (squares // 2), head, matrix].astype(jnp.float32)
                out_ref[to, slot] = (old - updates[slot, pl.ds(at, rows), :]).astype(out_ref.dtype)


def square_body(queries, key_vectors, value_vectors, token_rates, fast_weights, squares):
    row_count = queries.shape[0]
    own_rows, _, num_heads, head_size = fast_weights.shape
    heads = num_heads // squares
    width = heads * head_size
    size = squares * PLACES
    half = size // 2
    hid = size * own_rows
    cut = squares // 2
    position = lax.axis_index("seq").astype(jnp.int32)
    spot = position % half // 2
    where = jnp.stack([spot, 2 * (position // half) + position % 2])
    params = pltpu.CompilerParams(vmem_limit_bytes=40 * 2**20)
    smem = pl.BlockSpec(memory_space=SMEM)
    vmem = pl.BlockSpec(memory_space=VMEM)

    def cost(mega_flops):
        return pl.CostEstimate(
            flops=mega_flops * 10**6, bytes_accessed=4 * 10**6, transcendentals=0
        )

    def swap(array, step):
        return lax.ppermute(array, "seq", [(at, at ^ step) for at in range(size)])

    def across(pieces):
        return [pieces[0]] + [swap(pieces[rel], 2 * rel) for rel in range(1, squares)]

    def bf16(*shape):
        return jax.ShapeDtypeStruct(shape, jnp.bfloat16)

    moved = across(
        pl.pallas_call(
            split_kernel,
            in_specs=[smem] + [vmem] * 4,
            out_specs=[vmem] * squares,
            out_shape=[bf16(3, row_count, width)] * squares,
            scratch_shapes=[VMEM((row_count, num_heads * head_size), jnp.bfloat16)],
            compiler_params=params,
            cost_estimate=cost(10),
            name="split",
        )(where, queries, key_vectors, value_vectors, token_rates)
    )

    by_spot = fast_weights.reshape(own_rows, 3, squares, heads, head_size).transpose(2, 3, 1, 0, 4)
    pieces = across(
        [
            lax.dynamic_index_in_dim(by_spot, spot ^ rel, 0, keepdims=False)
            for rel in range(squares)
        ]
    )
    own = [jnp.stack(pieces[:cut]), jnp.stack(pieces[cut:])]
    own = list(lax.optimization_barrier(own))
    other = [swap(w, half) for w in own]
    late, moved[2:] = lax.optimization_barrier((other, moved[2:]))
    weights = [own, [swap(w, 1) for w in own], other, [swap(w, 1) for w in late]]
    weights = [w for pair in weights for w in pair]

    weight_spec = pl.BlockSpec((cut, 1, 3, own_rows, head_size), lambda h: (0, h, 0, 0, 0))

    slots = -(-3 * heads // PLACES)
    sums_shape = (slots, hid, head_size)
    keep, near, far = pl.pallas_call(
        functools.partial(key_kernel, squares, heads),
        grid=(heads,),
        in_specs=[smem]
        + [pl.BlockSpec((2, row_count, head_size), lambda h: (0, 0, h))] * squares
        + [weight_spec] * 8,
        out_specs=[pl.BlockSpec((2, *sums_shape), lambda h: (0, 0, 0, 0))]
        + [pl.BlockSpec(sums_shape, lambda h: (0, 0, 0))] * 2,
        out_shape=[
            jax.ShapeDtypeStruct((2, *sums_shape), jnp.float32),
            bf16(*sums_shape),
            bf16(*sums_shape),
        ],
        scratch_shapes=[VMEM((3, hid, head_size), jnp.float32)],
        compiler_params=params,
        cost_estimate=cost(2000),
        name="key_side",
    )(where, *moved, *weights)

    near = swap(near, 1)
    far = swap((keep[1] + swap(far, 1).astype(jnp.float32)).astype(jnp.bfloat16), half)

    columns = pl.BlockSpec((row_count, head_size), lambda h: (0, h))
    parts = pl.pallas_call(
        functools.partial(query_kernel, squares),
        grid=(heads,),
        in_specs=[pl.BlockSpec((1, row_count, head_size), lambda h: (2, 0, h))] * squares
        + [weight_spec] * 8,
        out_specs=[columns] * squares,
        out_shape=[bf16(row_count, width)] * squares,
        compiler_params=params,
        cost_estimate=cost(1000),
        name="query_side",
    )(*moved, *weights)
    parts = across(parts)
    far, parts[2:] = lax.optimization_barrier((far, parts[2:]))
    applied = pl.pallas_call(
        join_kernel,
        in_specs=[smem] + [vmem] * squares,
        out_specs=vmem,
        out_shape=bf16(row_count, num_heads * head_size),
        compiler_params=params,
        cost_estimate=cost(10),
        name="join",
    )(where, *parts)

    renewed = pl.pallas_call(
        functools.partial(renew_kernel, squares),
        in_specs=[smem] + [vmem] * 11,
        out_specs=vmem,
        out_shape=bf16(size, slots, own_rows, head_size),
        scratch_shapes=[VMEM(sums_shape, jnp.float32)],
        compiler_params=params,
        cost_estimate=cost(2000),
        name="renew",
    )(where, keep, near, far, *weights)
    back = lax.all_to_all(renewed, "seq", 0, 0, tiled=True)
    back = back.reshape(2, squares, 2, slots, own_rows, head_size).transpose(1, 3, 0, 2, 4, 5)
    back = back.reshape(squares, PLACES * slots, own_rows, head_size)[:, : 3 * heads]
    renewed_out = (
        back.reshape(squares, heads, 3, own_rows, head_size)
        .transpose(3, 2, 0, 1, 4)
        .reshape(own_rows, 3, num_heads, head_size)
    )
    return applied, renewed_out


def newton_factor(gram_matrix):
    exact = lax.Precision.HIGHEST
    head_size = gram_matrix.shape[-1]
    trace_sum = jnp.trace(gram_matrix, axis1=-2, axis2=-1)
    factor = 1.0 / (jnp.sqrt(trace_sum) + 1e-07)
    poly_factor = factor[..., None, None] * jnp.eye(head_size, dtype=jnp.float32)
    for newton_step in range(NS_STEPS):
        inner_term = jnp.matmul(gram_matrix, poly_factor, precision=exact)
        square = jnp.matmul(poly_factor, inner_term, precision=exact)
        mixed_term = coef_b * square + coef_c * jnp.matmul(square, square, precision=exact)
        poly_factor = coef_a * poly_factor + jnp.matmul(mixed_term, poly_factor, precision=exact)
    return poly_factor


def hidden_block(query_heads, key_heads, scaled_v, weight_block):
    head_size = query_heads.shape[2]
    scale_in = 1.0 / math.sqrt(head_size)
    scale_out = 1.0 / math.sqrt(HID)
    query_first = scale_in * jnp.einsum(
        "thd,jhd->thj", query_heads, weight_block[:, 0], preferred_element_type=jnp.float32
    )
    query_third = scale_in * jnp.einsum(
        "thd,jhd->thj", query_heads, weight_block[:, 1], preferred_element_type=jnp.float32
    )
    hidden_q = (query_first * jax.nn.sigmoid(query_first) * query_third).astype(jnp.bfloat16)
    partial_out = scale_out * jnp.einsum(
        "thj,jhd->thd", hidden_q, weight_block[:, 2], preferred_element_type=jnp.float32
    )
    key_first = scale_in * jnp.einsum(
        "thd,jhd->thj", key_heads, weight_block[:, 0], preferred_element_type=jnp.float32
    )
    key_third = scale_in * jnp.einsum(
        "thd,jhd->thj", key_heads, weight_block[:, 1], preferred_element_type=jnp.float32
    )
    sigmoid_k = jax.nn.sigmoid(key_first)
    activated = key_first * sigmoid_k
    hidden_k = (activated * key_third).astype(jnp.bfloat16)
    back_grad = jnp.einsum(
        "thd,jhd->thj", scaled_v, weight_block[:, 2], preferred_element_type=jnp.float32
    )
    grad_third = (back_grad * activated).astype(jnp.bfloat16)
    grad_first = (back_grad * key_third * sigmoid_k * (1.0 + key_first * (1.0 - sigmoid_k))).astype(
        jnp.bfloat16
    )
    return (partial_out, hidden_k, grad_first, grad_third)


def gather_body(queries, key_vectors, value_vectors, token_rates, fast_weights):
    exact = lax.Precision.HIGHEST
    row_count = queries.shape[0]
    num_heads = fast_weights.shape[2]
    head_size = fast_weights.shape[3]
    scale_in = 1.0 / math.sqrt(head_size)
    scale_out = 1.0 / math.sqrt(HID)
    query_heads = queries.reshape(row_count, num_heads, head_size)
    key_heads = key_vectors.reshape(row_count, num_heads, head_size)
    value_heads = value_vectors.reshape(row_count, num_heads, head_size)
    scaled_v = (-scale_out * token_rates[:, :, None] * value_heads.astype(jnp.float32)).astype(
        jnp.bfloat16
    )
    gathered = lax.all_gather(fast_weights, "seq", axis=0, tiled=True)
    out_sum, hidden_k, grad_first, grad_third = hidden_block(
        query_heads, key_heads, scaled_v, gathered
    )
    applied = out_sum.astype(jnp.bfloat16).reshape(row_count, num_heads * head_size)
    terms = (
        scale_in
        * jnp.einsum("thj,thd->jhd", grad_first, key_heads, preferred_element_type=jnp.float32),
        scale_in
        * jnp.einsum("thj,thd->jhd", grad_third, key_heads, preferred_element_type=jnp.float32),
        jnp.einsum("thj,thd->jhd", hidden_k, scaled_v, preferred_element_type=jnp.float32),
    )
    sums = [
        jnp.sum(
            lax.all_to_all(term[:, None], "seq", split_axis=0, concat_axis=1, tiled=True), axis=1
        )
        for term in terms
    ]
    gradient = jnp.stack(sums, axis=1)
    partial_gram = jnp.einsum("jmhd,jmhe->mhde", gradient, gradient, precision=exact)
    gram_matrix = lax.psum(partial_gram, "seq")
    poly_factor = newton_factor(gram_matrix)
    update = jnp.einsum("mhde,jmhe->jmhd", poly_factor, gradient, precision=exact)
    renewed = (fast_weights.astype(jnp.float32) - math.sqrt(HID) * update).astype(jnp.bfloat16)
    return (applied, renewed)


def body(size, queries, key_vectors, value_vectors, token_rates, fast_weights):
    squares = size // PLACES
    if (
        size == PLACES * squares
        and squares > 1
        and squares & (squares - 1) == 0
        and fast_weights.shape[2] % squares == 0
    ):
        return square_body(
            queries, key_vectors, value_vectors, token_rates, fast_weights, squares
        )
    return gather_body(queries, key_vectors, value_vectors, token_rates, fast_weights)


def solution(mesh):
    in_specs = (
        P(("groups", "seq"), None),
        P(("groups", "seq"), None),
        P(("groups", "seq"), None),
        P(("groups", "seq"), None),
        P(("groups", "seq"), None, None, None),
    )
    out_specs = (P(("groups", "seq"), None), P(("groups", "seq"), None, None, None))
    return jax.shard_map(
        functools.partial(body, mesh.shape["seq"]),
        mesh=mesh,
        in_specs=in_specs,
        out_specs=out_specs,
        check_vma=False,
    )
```

```python
import functools
import math

import jax
import jax.numpy as jnp
from jax import lax
from jax.experimental import pallas as pl
from jax.experimental.pallas import tpu as pltpu
from jax.sharding import PartitionSpec as P

HID = 512
NS_STEPS = 2
PLACES = 4

coef_a = 3.4445
coef_b = -4.775
coef_c = 2.0315

VMEM = pltpu.VMEM
SMEM = pltpu.SMEM
NT = (((1,), (1,)), ((), ()))
NN = (((1,), (0,)), ((), ()))
TN = (((0,), (0,)), ((), ()))


def dot(a, b, dims, precision=None):
    return lax.dot_general(a, b, dims, precision=precision, preferred_element_type=jnp.float32)


def split_kernel(where_ref, q_ref, k_ref, v_ref, rate_ref, *refs):
    outs, scaled = refs[:-1], refs[-1]
    spot = where_ref[0]
    squares = len(outs) // 2
    width = outs[0].shape[2]
    num_heads = rate_ref.shape[1]
    head_size = k_ref.shape[1] // num_heads
    rates = (-1.0 / math.sqrt(HID)) * rate_ref[...]
    for head in range(num_heads):
        at = slice(head * head_size, (head + 1) * head_size)
        scaled[:, at] = (rates[:, head : head + 1] * v_ref[:, at].astype(jnp.float32)).astype(
            jnp.bfloat16
        )
    for rel in range(squares):
        at = pl.multiple_of((spot ^ rel) * width, width)
        outs[rel][0] = k_ref[:, pl.ds(at, width)]
        outs[rel][1] = scaled[:, pl.ds(at, width)]
        outs[squares + rel][...] = q_ref[:, pl.ds(at, width)]


def join_kernel(where_ref, *refs):
    ins, out_ref = refs[:-1], refs[-1]
    spot = where_ref[0]
    width = ins[0].shape[1]
    for rel, in_ref in enumerate(ins):
        at = pl.multiple_of((spot ^ rel) * width, width)
        out_ref[:, pl.ds(at, width)] = in_ref[...]


def weight_rows(w_refs, rel, matrix):
    pieces = w_refs[2 * rel : 2 * rel + 2]
    return jnp.concatenate(
        [w[at, 0, matrix] for w in pieces for at in range(w.shape[0])], axis=0
    )


def key_kernel(squares, heads, where_ref, *refs):
    pairs, w_refs = refs[:squares], refs[squares : squares + 8]
    keep_ref, near_ref, *far_refs, terms = refs[squares + 8 :]
    spot, place = where_ref[0], where_ref[1]
    _, hid, head_size = terms.shape
    rows = hid // (PLACES * squares)
    step = pl.program_id(0)
    scale_in = 1.0 / math.sqrt(head_size)

    def put(number, value):
        rel = (number % PLACES) ^ place
        slot = number // PLACES

        @pl.when(rel % 2 == 0)
        def _():
            keep_ref[rel // 2, slot] = value

        @pl.when(rel == 1)
        def _():
            near_ref[slot] = value.astype(near_ref.dtype)

        for one, far_ref in enumerate(far_refs):

            @pl.when((rel == 3) & (slot == one))
            def _():
                far_ref[...] = value.astype(far_ref.dtype)

    @pl.when(step == 0)
    def _():
        for number in range(3 * heads, PLACES * keep_ref.shape[1]):
            put(number, jnp.zeros((hid, head_size), jnp.float32))

    keys = jnp.concatenate([pair[0] for pair in pairs], axis=0)
    scaled = jnp.concatenate([pair[1] for pair in pairs], axis=0)
    both_maps = jnp.concatenate(
        [weight_rows(w_refs, rel, matrix) for matrix in range(2) for rel in range(PLACES)], axis=0
    )
    second = jnp.concatenate([weight_rows(w_refs, rel, 2) for rel in range(PLACES)], axis=0)
    raw = dot(both_maps, keys, NT)
    third = raw[hid:] * scale_in
    back = dot(second, scaled, NT)
    half_first = raw[:hid] * (0.5 * scale_in)
    tanh = jnp.tanh(half_first)
    act = half_first + half_first * tanh
    hidden = (act * third).astype(jnp.bfloat16)
    grad_third = (back * act).astype(jnp.bfloat16)
    twice_slope = (1.0 + tanh) + act * (1.0 - tanh)
    grad_first = (back * third * twice_slope).astype(jnp.bfloat16)
    firsts = dot(jnp.concatenate([grad_first, grad_third], axis=0), keys, NN)
    values = (
        firsts[:hid] * (0.5 * scale_in),
        firsts[hid:] * scale_in,
        dot(hidden, scaled, NN),
    )
    for rel in range(PLACES):
        for apart in range(squares):
            at = (rel * squares + apart) * rows
            to = pl.multiple_of(((place ^ rel) * squares + (spot ^ apart)) * rows, rows)
            for matrix in range(3):
                terms[matrix, pl.ds(to, rows), :] = values[matrix][at : at + rows]
    for matrix in range(3):
        put(3 * step + matrix, terms[matrix])


def query_kernel(squares, *refs):
    ins, w_refs, outs = refs[:squares], refs[squares : squares + 8], refs[-squares:]
    scale_in = 1.0 / math.sqrt(ins[0].shape[1])
    scale_out = 1.0 / math.sqrt(HID)
    first_map, third_map, second = (
        jnp.concatenate([weight_rows(w_refs, rel, matrix) for rel in range(PLACES)], axis=0)
        for matrix in range(3)
    )
    queries = jnp.concatenate([q_ref[...] for q_ref in ins], axis=0)
    half_first = dot(queries, first_map, NT) * (0.5 * scale_in)
    third = dot(queries, third_map, NT) * scale_in
    hidden = ((half_first + half_first * jnp.tanh(half_first)) * third).astype(jnp.bfloat16)
    out = (dot(hidden, second, NN) * scale_out).astype(jnp.bfloat16)
    rows = outs[0].shape[0]
    for rel, out_ref in enumerate(outs):
        out_ref[...] = out[rel * rows : (rel + 1) * rows]


def halves(array):
    high = array.astype(jnp.bfloat16)
    return high, (array - high.astype(jnp.float32)).astype(jnp.bfloat16)


def dot_halves(a, b, dims):
    return dot(a[0], b[0], dims) + (dot(a[0], b[1], dims) + dot(a[1], b[0], dims))


def renew_kernel(squares, where_ref, mine_ref, near_ref, far_ref, *refs):
    w_refs, (out_ref, updates) = refs[:8], refs[-2:]
    spot, place = where_ref[0], where_ref[1]
    slots, hid, head_size = far_ref.shape
    heads = w_refs[0].shape[1]
    rows = out_ref.shape[2]
    eye = (
        lax.broadcasted_iota(jnp.int32, (head_size, head_size), 0)
        == lax.broadcasted_iota(jnp.int32, (head_size, head_size), 1)
    ).astype(jnp.float32)
    grads = [
        mine_ref[0, slot]
        + near_ref[slot].astype(jnp.float32)
        + far_ref[slot].astype(jnp.float32)
        for slot in range(slots)
    ]
    grads = [halves(grad) for grad in grads]
    grams = []
    for high, low in grads:
        cross = dot(high, low, TN)
        grams.append(dot(high, high, TN) + (cross + cross.T))
    scales = [1.0 / (jnp.sqrt(jnp.sum(gram * eye)) + 1e-07) for gram in grams]
    factors = []
    for gram, scale in zip(grams, scales):
        square = (scale * scale) * gram
        parts = halves(square)
        factors.append(
            scale * (coef_a * eye + coef_b * square + coef_c * dot_halves(parts, parts, NN))
        )
    grams = [halves(gram) for gram in grams]
    for _ in range(NS_STEPS - 1):
        parts = [halves(factor) for factor in factors]
        inner = [dot_halves(gram, part, NN) for gram, part in zip(grams, parts)]
        squares_of = [dot_halves(part, halves(term), NN) for part, term in zip(parts, inner)]
        mixed = []
        for square in squares_of:
            term = halves(square)
            mixed.append(coef_b * square + coef_c * dot_halves(term, term, NN))
        factors = [
            coef_a * factor + dot_halves(halves(term), part, NN)
            for term, factor, part in zip(mixed, factors, parts)
        ]
    for slot in range(slots):
        updates[slot] = math.sqrt(HID) * dot_halves(grads[slot], halves(factors[slot]), NT)
    for slot in range(slots):
        number = jnp.minimum(PLACES * slot + place, 3 * heads - 1)
        head, matrix = number // 3, number % 3
        for rel in range(PLACES):
            owner = place ^ rel
            for apart in range(squares):
                w = w_refs[2 * rel + apart // (squares // 2)]
                at = pl.multiple_of((owner * squares + (spot ^ apart)) * rows, rows)
                to = (owner // 2 * squares + (spot ^ apart)) * 2 + owner % 2
                old = w[apart % (squares // 2), head, matrix].astype(jnp.float32)
                out_ref[to, slot] = (old - updates[slot, pl.ds(at, rows), :]).astype(out_ref.dtype)


def square_body(queries, key_vectors, value_vectors, token_rates, fast_weights, squares):
    row_count = queries.shape[0]
    own_rows, _, num_heads, head_size = fast_weights.shape
    heads = num_heads // squares
    width = heads * head_size
    size = squares * PLACES
    half = size // 2
    hid = size * own_rows
    cut = squares // 2
    position = lax.axis_index("seq").astype(jnp.int32)
    spot = position % half // 2
    where = jnp.stack([spot, 2 * (position // half) + position % 2])
    params = pltpu.CompilerParams(vmem_limit_bytes=40 * 2**20)
    smem = pl.BlockSpec(memory_space=SMEM)
    vmem = pl.BlockSpec(memory_space=VMEM)

    def cost(mega_flops):
        return pl.CostEstimate(
            flops=mega_flops * 10**6, bytes_accessed=4 * 10**6, transcendentals=0
        )

    def swap(array, step):
        return lax.ppermute(array, "seq", [(at, at ^ step) for at in range(size)])

    def across(pieces):
        return [pieces[0]] + [swap(pieces[rel], 2 * rel) for rel in range(1, squares)]

    def bf16(*shape):
        return jax.ShapeDtypeStruct(shape, jnp.bfloat16)

    pieces = pl.pallas_call(
        split_kernel,
        in_specs=[smem] + [vmem] * 4,
        out_specs=[vmem] * (2 * squares),
        out_shape=[bf16(2, row_count, width)] * squares + [bf16(row_count, width)] * squares,
        scratch_shapes=[VMEM((row_count, num_heads * head_size), jnp.bfloat16)],
        compiler_params=params,
        cost_estimate=cost(10),
        name="split",
    )(where, queries, key_vectors, value_vectors, token_rates)
    moved, asking = across(pieces[:squares]), pieces[squares:]

    by_spot = fast_weights.reshape(own_rows, 3, squares, heads, head_size).transpose(2, 3, 1, 0, 4)
    pieces = across(
        [
            lax.dynamic_index_in_dim(by_spot, spot ^ rel, 0, keepdims=False)
            for rel in range(squares)
        ]
    )
    own = [jnp.stack(pieces[:cut]), jnp.stack(pieces[cut:])]
    own = list(lax.optimization_barrier(own))
    other = [swap(w, half) for w in own]
    late, moved[2:] = lax.optimization_barrier((other, moved[2:]))
    other, asking = lax.optimization_barrier((other, asking))
    asking = across(asking)
    weights = [own, [swap(w, 1) for w in own], other, [swap(w, 1) for w in late]]
    weights = [w for pair in weights for w in pair]

    weight_spec = pl.BlockSpec((cut, 1, 3, own_rows, head_size), lambda h: (0, h, 0, 0, 0))

    slots = -(-3 * heads // PLACES)
    sums_shape = (slots, hid, head_size)
    keep, near, *far = pl.pallas_call(
        functools.partial(key_kernel, squares, heads),
        grid=(heads,),
        in_specs=[smem]
        + [pl.BlockSpec((2, row_count, head_size), lambda h: (0, 0, h))] * squares
        + [weight_spec] * 8,
        out_specs=[pl.BlockSpec((2, *sums_shape), lambda h: (0, 0, 0, 0))]
        + [pl.BlockSpec(sums_shape, lambda h: (0, 0, 0))]
        + [pl.BlockSpec(sums_shape[1:], lambda h: (0, 0))] * slots,
        out_shape=[
            jax.ShapeDtypeStruct((2, *sums_shape), jnp.float32),
            bf16(*sums_shape),
            *[bf16(*sums_shape[1:])] * slots,
        ],
        scratch_shapes=[VMEM((3, hid, head_size), jnp.float32)],
        compiler_params=params,
        cost_estimate=cost(2000),
        name="key_side",
    )(where, *moved, *weights)

    near = swap(near, 1)
    far = [swap(one, 1) for one in far]
    far, asking = lax.optimization_barrier((far, asking))
    far = jnp.stack(far).astype(jnp.float32)
    far = swap((keep[1] + far).astype(jnp.bfloat16), half)

    columns = pl.BlockSpec((row_count, head_size), lambda h: (0, h))
    parts = pl.pallas_call(
        functools.partial(query_kernel, squares),
        grid=(heads,),
        in_specs=[columns] * squares
        + [weight_spec] * 8,
        out_specs=[columns] * squares,
        out_shape=[bf16(row_count, width)] * squares,
        compiler_params=params,
        cost_estimate=cost(1000),
        name="query_side",
    )(*asking, *weights)
    parts = across(parts)
    far, parts[2:] = lax.optimization_barrier((far, parts[2:]))
    applied = pl.pallas_call(
        join_kernel,
        in_specs=[smem] + [vmem] * squares,
        out_specs=vmem,
        out_shape=bf16(row_count, num_heads * head_size),
        compiler_params=params,
        cost_estimate=cost(10),
        name="join",
    )(where, *parts)

    renewed = pl.pallas_call(
        functools.partial(renew_kernel, squares),
        in_specs=[smem] + [vmem] * 11,
        out_specs=vmem,
        out_shape=bf16(size, slots, own_rows, head_size),
        scratch_shapes=[VMEM(sums_shape, jnp.float32)],
        compiler_params=params,
        cost_estimate=cost(2000),
        name="renew",
    )(where, keep, near, far, *weights)
    back = lax.all_to_all(renewed, "seq", 0, 0, tiled=True)
    back = back.reshape(2, squares, 2, slots, own_rows, head_size).transpose(1, 3, 0, 2, 4, 5)
    back = back.reshape(squares, PLACES * slots, own_rows, head_size)[:, : 3 * heads]
    renewed_out = (
        back.reshape(squares, heads, 3, own_rows, head_size)
        .transpose(3, 2, 0, 1, 4)
        .reshape(own_rows, 3, num_heads, head_size)
    )
    return applied, renewed_out


def newton_factor(gram_matrix):
    exact = lax.Precision.HIGHEST
    head_size = gram_matrix.shape[-1]
    trace_sum = jnp.trace(gram_matrix, axis1=-2, axis2=-1)
    factor = 1.0 / (jnp.sqrt(trace_sum) + 1e-07)
    poly_factor = factor[..., None, None] * jnp.eye(head_size, dtype=jnp.float32)
    for newton_step in range(NS_STEPS):
        inner_term = jnp.matmul(gram_matrix, poly_factor, precision=exact)
        square = jnp.matmul(poly_factor, inner_term, precision=exact)
        mixed_term = coef_b * square + coef_c * jnp.matmul(square, square, precision=exact)
        poly_factor = coef_a * poly_factor + jnp.matmul(mixed_term, poly_factor, precision=exact)
    return poly_factor


def hidden_block(query_heads, key_heads, scaled_v, weight_block):
    head_size = query_heads.shape[2]
    scale_in = 1.0 / math.sqrt(head_size)
    scale_out = 1.0 / math.sqrt(HID)
    query_first = scale_in * jnp.einsum(
        "thd,jhd->thj", query_heads, weight_block[:, 0], preferred_element_type=jnp.float32
    )
    query_third = scale_in * jnp.einsum(
        "thd,jhd->thj", query_heads, weight_block[:, 1], preferred_element_type=jnp.float32
    )
    hidden_q = (query_first * jax.nn.sigmoid(query_first) * query_third).astype(jnp.bfloat16)
    partial_out = scale_out * jnp.einsum(
        "thj,jhd->thd", hidden_q, weight_block[:, 2], preferred_element_type=jnp.float32
    )
    key_first = scale_in * jnp.einsum(
        "thd,jhd->thj", key_heads, weight_block[:, 0], preferred_element_type=jnp.float32
    )
    key_third = scale_in * jnp.einsum(
        "thd,jhd->thj", key_heads, weight_block[:, 1], preferred_element_type=jnp.float32
    )
    sigmoid_k = jax.nn.sigmoid(key_first)
    activated = key_first * sigmoid_k
    hidden_k = (activated * key_third).astype(jnp.bfloat16)
    back_grad = jnp.einsum(
        "thd,jhd->thj", scaled_v, weight_block[:, 2], preferred_element_type=jnp.float32
    )
    grad_third = (back_grad * activated).astype(jnp.bfloat16)
    grad_first = (back_grad * key_third * sigmoid_k * (1.0 + key_first * (1.0 - sigmoid_k))).astype(
        jnp.bfloat16
    )
    return (partial_out, hidden_k, grad_first, grad_third)


def gather_body(queries, key_vectors, value_vectors, token_rates, fast_weights):
    exact = lax.Precision.HIGHEST
    row_count = queries.shape[0]
    num_heads = fast_weights.shape[2]
    head_size = fast_weights.shape[3]
    scale_in = 1.0 / math.sqrt(head_size)
    scale_out = 1.0 / math.sqrt(HID)
    query_heads = queries.reshape(row_count, num_heads, head_size)
    key_heads = key_vectors.reshape(row_count, num_heads, head_size)
    value_heads = value_vectors.reshape(row_count, num_heads, head_size)
    scaled_v = (-scale_out * token_rates[:, :, None] * value_heads.astype(jnp.float32)).astype(
        jnp.bfloat16
    )
    gathered = lax.all_gather(fast_weights, "seq", axis=0, tiled=True)
    out_sum, hidden_k, grad_first, grad_third = hidden_block(
        query_heads, key_heads, scaled_v, gathered
    )
    applied = out_sum.astype(jnp.bfloat16).reshape(row_count, num_heads * head_size)
    terms = (
        scale_in
        * jnp.einsum("thj,thd->jhd", grad_first, key_heads, preferred_element_type=jnp.float32),
        scale_in
        * jnp.einsum("thj,thd->jhd", grad_third, key_heads, preferred_element_type=jnp.float32),
        jnp.einsum("thj,thd->jhd", hidden_k, scaled_v, preferred_element_type=jnp.float32),
    )
    sums = [
        jnp.sum(
            lax.all_to_all(term[:, None], "seq", split_axis=0, concat_axis=1, tiled=True), axis=1
        )
        for term in terms
    ]
    gradient = jnp.stack(sums, axis=1)
    partial_gram = jnp.einsum("jmhd,jmhe->mhde", gradient, gradient, precision=exact)
    gram_matrix = lax.psum(partial_gram, "seq")
    poly_factor = newton_factor(gram_matrix)
    update = jnp.einsum("mhde,jmhe->jmhd", poly_factor, gradient, precision=exact)
    renewed = (fast_weights.astype(jnp.float32) - math.sqrt(HID) * update).astype(jnp.bfloat16)
    return (applied, renewed)


def body(size, queries, key_vectors, value_vectors, token_rates, fast_weights):
    squares = size // PLACES
    if (
        size == PLACES * squares
        and squares > 1
        and squares & (squares - 1) == 0
        and fast_weights.shape[2] % squares == 0
    ):
        return square_body(
            queries, key_vectors, value_vectors, token_rates, fast_weights, squares
        )
    return gather_body(queries, key_vectors, value_vectors, token_rates, fast_weights)


def solution(mesh):
    in_specs = (
        P(("groups", "seq"), None),
        P(("groups", "seq"), None),
        P(("groups", "seq"), None),
        P(("groups", "seq"), None),
        P(("groups", "seq"), None, None, None),
    )
    out_specs = (P(("groups", "seq"), None), P(("groups", "seq"), None, None, None))
    return jax.shard_map(
        functools.partial(body, mesh.shape["seq"]),
        mesh=mesh,
        in_specs=in_specs,
        out_specs=out_specs,
        check_vma=False,
    )
```

```python
import functools
import math

import jax
import jax.numpy as jnp
from jax import lax
from jax.experimental import pallas as pl
from jax.experimental.pallas import tpu as pltpu
from jax.sharding import PartitionSpec as P

HID = 512
NS_STEPS = 2
PLACES = 4

coef_a = 3.4445
coef_b = -4.775
coef_c = 2.0315

VMEM = pltpu.VMEM
SMEM = pltpu.SMEM
NT = (((1,), (1,)), ((), ()))
NN = (((1,), (0,)), ((), ()))
TN = (((0,), (0,)), ((), ()))


def dot(a, b, dims, precision=None):
    return lax.dot_general(a, b, dims, precision=precision, preferred_element_type=jnp.float32)


def split_kernel(where_ref, q_ref, k_ref, v_ref, rate_ref, *refs):
    outs, scaled = refs[:-1], refs[-1]
    spot = where_ref[0]
    squares = len(outs) // 2
    width = outs[0].shape[2]
    num_heads = rate_ref.shape[1]
    head_size = k_ref.shape[1] // num_heads
    rates = (-1.0 / math.sqrt(HID)) * rate_ref[...]
    for head in range(num_heads):
        at = slice(head * head_size, (head + 1) * head_size)
        scaled[:, at] = (rates[:, head : head + 1] * v_ref[:, at].astype(jnp.float32)).astype(
            jnp.bfloat16
        )
    for rel in range(squares):
        at = pl.multiple_of((spot ^ rel) * width, width)
        outs[rel][0] = k_ref[:, pl.ds(at, width)]
        outs[rel][1] = scaled[:, pl.ds(at, width)]
        outs[squares + rel][...] = q_ref[:, pl.ds(at, width)]


def join_kernel(where_ref, *refs):
    ins, out_ref = refs[:-1], refs[-1]
    spot = where_ref[0]
    width = ins[0].shape[1]
    for rel, in_ref in enumerate(ins):
        at = pl.multiple_of((spot ^ rel) * width, width)
        out_ref[:, pl.ds(at, width)] = in_ref[...]


def weight_rows(w_refs, rel, matrix):
    pieces = w_refs[2 * rel : 2 * rel + 2]
    return jnp.concatenate(
        [w[at, 0, matrix] for w in pieces for at in range(w.shape[0])], axis=0
    )


def key_kernel(squares, heads, where_ref, *refs):
    pairs, w_refs = refs[:squares], refs[squares : squares + 8]
    mine_ref, sent_ref, near_ref, *far_refs, terms = refs[squares + 8 :]
    spot, place = where_ref[0], where_ref[1]
    _, hid, head_size = terms.shape
    rows = hid // (PLACES * squares)
    step = pl.program_id(0)
    scale_in = 1.0 / math.sqrt(head_size)

    def put(number, value):
        rel = (number % PLACES) ^ place
        slot = number // PLACES

        @pl.when(rel == 0)
        def _():
            mine_ref[slot] = value

        @pl.when(rel == 2)
        def _():
            sent_ref[slot] = value

        @pl.when(rel == 1)
        def _():
            near_ref[slot] = value.astype(near_ref.dtype)

        for one, far_ref in enumerate(far_refs):

            @pl.when((rel == 3) & (slot == one))
            def _():
                far_ref[...] = value.astype(far_ref.dtype)

    @pl.when(step == 0)
    def _():
        for number in range(3 * heads, PLACES * mine_ref.shape[0]):
            put(number, jnp.zeros((hid, head_size), jnp.float32))

    keys = jnp.concatenate([pair[0] for pair in pairs], axis=0)
    scaled = jnp.concatenate([pair[1] for pair in pairs], axis=0)
    both_maps = jnp.concatenate(
        [weight_rows(w_refs, rel, matrix) for matrix in range(2) for rel in range(PLACES)], axis=0
    )
    second = jnp.concatenate([weight_rows(w_refs, rel, 2) for rel in range(PLACES)], axis=0)
    raw = dot(both_maps, keys, NT)
    third = raw[hid:] * scale_in
    back = dot(second, scaled, NT)
    half_first = raw[:hid] * (0.5 * scale_in)
    tanh = jnp.tanh(half_first)
    act = half_first + half_first * tanh
    hidden = (act * third).astype(jnp.bfloat16)
    grad_third = (back * act).astype(jnp.bfloat16)
    twice_slope = (1.0 + tanh) + act * (1.0 - tanh)
    grad_first = (back * third * twice_slope).astype(jnp.bfloat16)
    firsts = dot(jnp.concatenate([grad_first, grad_third], axis=0), keys, NN)
    values = (
        firsts[:hid] * (0.5 * scale_in),
        firsts[hid:] * scale_in,
        dot(hidden, scaled, NN),
    )
    for rel in range(PLACES):
        for apart in range(squares):
            at = (rel * squares + apart) * rows
            to = pl.multiple_of(((place ^ rel) * squares + (spot ^ apart)) * rows, rows)
            for matrix in range(3):
                terms[matrix, pl.ds(to, rows), :] = values[matrix][at : at + rows]
    for matrix in range(3):
        put(3 * step + matrix, terms[matrix])


def query_kernel(squares, *refs):
    ins, w_refs, outs = refs[:squares], refs[squares : squares + 8], refs[-squares:]
    scale_in = 1.0 / math.sqrt(ins[0].shape[1])
    scale_out = 1.0 / math.sqrt(HID)
    first_map, third_map, second = (
        jnp.concatenate([weight_rows(w_refs, rel, matrix) for rel in range(PLACES)], axis=0)
        for matrix in range(3)
    )
    queries = jnp.concatenate([q_ref[...] for q_ref in ins], axis=0)
    half_first = dot(queries, first_map, NT) * (0.5 * scale_in)
    third = dot(queries, third_map, NT) * scale_in
    hidden = ((half_first + half_first * jnp.tanh(half_first)) * third).astype(jnp.bfloat16)
    out = (dot(hidden, second, NN) * scale_out).astype(jnp.bfloat16)
    rows = outs[0].shape[0]
    for rel, out_ref in enumerate(outs):
        out_ref[...] = out[rel * rows : (rel + 1) * rows]


def halves(array):
    high = array.astype(jnp.bfloat16)
    return high, (array - high.astype(jnp.float32)).astype(jnp.bfloat16)


def dot_halves(a, b, dims):
    return dot(a[0], b[0], dims) + (dot(a[0], b[1], dims) + dot(a[1], b[0], dims))


def pick_kernel(squares, where_ref, *refs):
    w_refs, out_ref = refs[:8], refs[8]
    spot, place = where_ref[0], where_ref[1]
    heads = w_refs[0].shape[1]
    for slot in range(out_ref.shape[1]):
        number = jnp.minimum(PLACES * slot + place, 3 * heads - 1)
        for rel in range(PLACES):
            owner = place ^ rel
            for apart in range(squares):
                w = w_refs[2 * rel + apart // (squares // 2)]
                to = (owner // 2 * squares + (spot ^ apart)) * 2 + owner % 2
                out_ref[to, slot] = w[apart % (squares // 2), number // 3, number % 3]


def renew_kernel(squares, mine_ref, far_ref, old_ref, out_ref, updates):
    slots, hid, head_size = far_ref.shape
    rows = out_ref.shape[2]
    eye = (
        lax.broadcasted_iota(jnp.int32, (head_size, head_size), 0)
        == lax.broadcasted_iota(jnp.int32, (head_size, head_size), 1)
    ).astype(jnp.float32)
    grads = [
        mine_ref[slot]
        + far_ref[slot].astype(jnp.float32)
        for slot in range(slots)
    ]
    grads = [halves(grad) for grad in grads]
    grams = []
    for high, low in grads:
        cross = dot(high, low, TN)
        grams.append(dot(high, high, TN) + (cross + cross.T))
    scales = [1.0 / (jnp.sqrt(jnp.sum(gram * eye)) + 1e-07) for gram in grams]
    factors = []
    for gram, scale in zip(grams, scales):
        square = (scale * scale) * gram
        parts = halves(square)
        factors.append(
            scale * (coef_a * eye + coef_b * square + coef_c * dot_halves(parts, parts, NN))
        )
    grams = [halves(gram) for gram in grams]
    for _ in range(NS_STEPS - 1):
        parts = [halves(factor) for factor in factors]
        inner = [dot_halves(gram, part, NN) for gram, part in zip(grams, parts)]
        squares_of = [dot_halves(part, halves(term), NN) for part, term in zip(parts, inner)]
        mixed = []
        for square in squares_of:
            term = halves(square)
            mixed.append(coef_b * square + coef_c * dot_halves(term, term, NN))
        factors = [
            coef_a * factor + dot_halves(halves(term), part, NN)
            for term, factor, part in zip(mixed, factors, parts)
        ]
    for slot in range(slots):
        updates[slot] = math.sqrt(HID) * dot_halves(grads[slot], halves(factors[slot]), NT)
    for slot in range(slots):
        for owner in range(PLACES):
            for at in range(squares):
                to = (owner // 2 * squares + at) * 2 + owner % 2
                rows_at = slice((owner * squares + at) * rows, (owner * squares + at + 1) * rows)
                old = old_ref[to, slot].astype(jnp.float32)
                out_ref[to, slot] = (old - updates[slot, rows_at, :]).astype(out_ref.dtype)


def square_body(queries, key_vectors, value_vectors, token_rates, fast_weights, squares):
    row_count = queries.shape[0]
    own_rows, _, num_heads, head_size = fast_weights.shape
    heads = num_heads // squares
    width = heads * head_size
    size = squares * PLACES
    half = size // 2
    hid = size * own_rows
    cut = squares // 2
    position = lax.axis_index("seq").astype(jnp.int32)
    spot = position % half // 2
    where = jnp.stack([spot, 2 * (position // half) + position % 2])
    params = pltpu.CompilerParams(vmem_limit_bytes=40 * 2**20)
    smem = pl.BlockSpec(memory_space=SMEM)
    vmem = pl.BlockSpec(memory_space=VMEM)

    def cost(mega_flops):
        return pl.CostEstimate(
            flops=mega_flops * 10**6, bytes_accessed=4 * 10**6, transcendentals=0
        )

    def swap(array, step):
        return lax.ppermute(array, "seq", [(at, at ^ step) for at in range(size)])

    def across(pieces):
        return [pieces[0]] + [swap(pieces[rel], 2 * rel) for rel in range(1, squares)]

    def bf16(*shape):
        return jax.ShapeDtypeStruct(shape, jnp.bfloat16)

    pieces = pl.pallas_call(
        split_kernel,
        in_specs=[smem] + [vmem] * 4,
        out_specs=[vmem] * (2 * squares),
        out_shape=[bf16(2, row_count, width)] * squares + [bf16(row_count, width)] * squares,
        scratch_shapes=[VMEM((row_count, num_heads * head_size), jnp.bfloat16)],
        compiler_params=params,
        cost_estimate=cost(10),
        name="split",
    )(where, queries, key_vectors, value_vectors, token_rates)
    moved, asking = across(pieces[:squares]), pieces[squares:]

    by_spot = fast_weights.reshape(own_rows, 3, squares, heads, head_size).transpose(2, 3, 1, 0, 4)
    pieces = across(
        [
            lax.dynamic_index_in_dim(by_spot, spot ^ rel, 0, keepdims=False)
            for rel in range(squares)
        ]
    )
    own = [jnp.stack(pieces[:cut]), jnp.stack(pieces[cut:])]
    own = list(lax.optimization_barrier(own))
    other = [swap(w, half) for w in own]
    late, moved[2:] = lax.optimization_barrier((other, moved[2:]))
    other, asking = lax.optimization_barrier((other, asking))
    asking = across(asking)
    weights = [own, [swap(w, 1) for w in own], other, [swap(w, 1) for w in late]]
    weights = [w for pair in weights for w in pair]

    weight_spec = pl.BlockSpec((cut, 1, 3, own_rows, head_size), lambda h: (0, h, 0, 0, 0))

    slots = -(-3 * heads // PLACES)
    sums_shape = (slots, hid, head_size)
    mine, sent, near, *far = pl.pallas_call(
        functools.partial(key_kernel, squares, heads),
        grid=(heads,),
        in_specs=[smem]
        + [pl.BlockSpec((2, row_count, head_size), lambda h: (0, 0, h))] * squares
        + [weight_spec] * 8,
        out_specs=[pl.BlockSpec(sums_shape, lambda h: (0, 0, 0))] * 3
        + [pl.BlockSpec(sums_shape[1:], lambda h: (0, 0))] * slots,
        out_shape=[
            jax.ShapeDtypeStruct(sums_shape, jnp.float32),
            jax.ShapeDtypeStruct(sums_shape, jnp.float32),
            bf16(*sums_shape),
            *[bf16(*sums_shape[1:])] * slots,
        ],
        scratch_shapes=[VMEM((3, hid, head_size), jnp.float32)],
        compiler_params=params,
        cost_estimate=cost(2000),
        name="key_side",
    )(where, *moved, *weights)

    near = swap(near, 1)
    mine = mine + near.astype(jnp.float32)
    far = [swap(one, 1) for one in far]
    far, asking = lax.optimization_barrier((far, asking))
    far = jnp.stack(far).astype(jnp.float32)
    far = swap((sent + far).astype(jnp.bfloat16), half)

    columns = pl.BlockSpec((row_count, head_size), lambda h: (0, h))
    parts = pl.pallas_call(
        functools.partial(query_kernel, squares),
        grid=(heads,),
        in_specs=[columns] * squares
        + [weight_spec] * 8,
        out_specs=[columns] * squares,
        out_shape=[bf16(row_count, width)] * squares,
        compiler_params=params,
        cost_estimate=cost(1000),
        name="query_side",
    )(*asking, *weights)
    parts, late_weights = lax.optimization_barrier((parts, weights))
    parts = across(parts)
    far, parts[2:] = lax.optimization_barrier((far, parts[2:]))
    applied = pl.pallas_call(
        join_kernel,
        in_specs=[smem] + [vmem] * squares,
        out_specs=vmem,
        out_shape=bf16(row_count, num_heads * head_size),
        compiler_params=params,
        cost_estimate=cost(10),
        name="join",
    )(where, *parts)

    old = pl.pallas_call(
        functools.partial(pick_kernel, squares),
        in_specs=[smem] + [vmem] * 8,
        out_specs=vmem,
        out_shape=bf16(size, slots, own_rows, head_size),
        compiler_params=params,
        cost_estimate=cost(10),
        name="pick",
    )(where, *late_weights)
    renewed = pl.pallas_call(
        functools.partial(renew_kernel, squares),
        in_specs=[vmem] * 3,
        out_specs=vmem,
        out_shape=bf16(size, slots, own_rows, head_size),
        scratch_shapes=[VMEM(sums_shape, jnp.float32)],
        compiler_params=params,
        cost_estimate=cost(2000),
        name="renew",
    )(mine, far, old)
    back = lax.all_to_all(renewed, "seq", 0, 0, tiled=True)
    back = back.reshape(2, squares, 2, slots, own_rows, head_size).transpose(1, 3, 0, 2, 4, 5)
    back = back.reshape(squares, PLACES * slots, own_rows, head_size)[:, : 3 * heads]
    renewed_out = (
        back.reshape(squares, heads, 3, own_rows, head_size)
        .transpose(3, 2, 0, 1, 4)
        .reshape(own_rows, 3, num_heads, head_size)
    )
    return applied, renewed_out


def newton_factor(gram_matrix):
    exact = lax.Precision.HIGHEST
    head_size = gram_matrix.shape[-1]
    trace_sum = jnp.trace(gram_matrix, axis1=-2, axis2=-1)
    factor = 1.0 / (jnp.sqrt(trace_sum) + 1e-07)
    poly_factor = factor[..., None, None] * jnp.eye(head_size, dtype=jnp.float32)
    for newton_step in range(NS_STEPS):
        inner_term = jnp.matmul(gram_matrix, poly_factor, precision=exact)
        square = jnp.matmul(poly_factor, inner_term, precision=exact)
        mixed_term = coef_b * square + coef_c * jnp.matmul(square, square, precision=exact)
        poly_factor = coef_a * poly_factor + jnp.matmul(mixed_term, poly_factor, precision=exact)
    return poly_factor


def hidden_block(query_heads, key_heads, scaled_v, weight_block):
    head_size = query_heads.shape[2]
    scale_in = 1.0 / math.sqrt(head_size)
    scale_out = 1.0 / math.sqrt(HID)
    query_first = scale_in * jnp.einsum(
        "thd,jhd->thj", query_heads, weight_block[:, 0], preferred_element_type=jnp.float32
    )
    query_third = scale_in * jnp.einsum(
        "thd,jhd->thj", query_heads, weight_block[:, 1], preferred_element_type=jnp.float32
    )
    hidden_q = (query_first * jax.nn.sigmoid(query_first) * query_third).astype(jnp.bfloat16)
    partial_out = scale_out * jnp.einsum(
        "thj,jhd->thd", hidden_q, weight_block[:, 2], preferred_element_type=jnp.float32
    )
    key_first = scale_in * jnp.einsum(
        "thd,jhd->thj", key_heads, weight_block[:, 0], preferred_element_type=jnp.float32
    )
    key_third = scale_in * jnp.einsum(
        "thd,jhd->thj", key_heads, weight_block[:, 1], preferred_element_type=jnp.float32
    )
    sigmoid_k = jax.nn.sigmoid(key_first)
    activated = key_first * sigmoid_k
    hidden_k = (activated * key_third).astype(jnp.bfloat16)
    back_grad = jnp.einsum(
        "thd,jhd->thj", scaled_v, weight_block[:, 2], preferred_element_type=jnp.float32
    )
    grad_third = (back_grad * activated).astype(jnp.bfloat16)
    grad_first = (back_grad * key_third * sigmoid_k * (1.0 + key_first * (1.0 - sigmoid_k))).astype(
        jnp.bfloat16
    )
    return (partial_out, hidden_k, grad_first, grad_third)


def gather_body(queries, key_vectors, value_vectors, token_rates, fast_weights):
    exact = lax.Precision.HIGHEST
    row_count = queries.shape[0]
    num_heads = fast_weights.shape[2]
    head_size = fast_weights.shape[3]
    scale_in = 1.0 / math.sqrt(head_size)
    scale_out = 1.0 / math.sqrt(HID)
    query_heads = queries.reshape(row_count, num_heads, head_size)
    key_heads = key_vectors.reshape(row_count, num_heads, head_size)
    value_heads = value_vectors.reshape(row_count, num_heads, head_size)
    scaled_v = (-scale_out * token_rates[:, :, None] * value_heads.astype(jnp.float32)).astype(
        jnp.bfloat16
    )
    gathered = lax.all_gather(fast_weights, "seq", axis=0, tiled=True)
    out_sum, hidden_k, grad_first, grad_third = hidden_block(
        query_heads, key_heads, scaled_v, gathered
    )
    applied = out_sum.astype(jnp.bfloat16).reshape(row_count, num_heads * head_size)
    terms = (
        scale_in
        * jnp.einsum("thj,thd->jhd", grad_first, key_heads, preferred_element_type=jnp.float32),
        scale_in
        * jnp.einsum("thj,thd->jhd", grad_third, key_heads, preferred_element_type=jnp.float32),
        jnp.einsum("thj,thd->jhd", hidden_k, scaled_v, preferred_element_type=jnp.float32),
    )
    sums = [
        jnp.sum(
            lax.all_to_all(term[:, None], "seq", split_axis=0, concat_axis=1, tiled=True), axis=1
        )
        for term in terms
    ]
    gradient = jnp.stack(sums, axis=1)
    partial_gram = jnp.einsum("jmhd,jmhe->mhde", gradient, gradient, precision=exact)
    gram_matrix = lax.psum(partial_gram, "seq")
    poly_factor = newton_factor(gram_matrix)
    update = jnp.einsum("mhde,jmhe->jmhd", poly_factor, gradient, precision=exact)
    renewed = (fast_weights.astype(jnp.float32) - math.sqrt(HID) * update).astype(jnp.bfloat16)
    return (applied, renewed)


def body(size, queries, key_vectors, value_vectors, token_rates, fast_weights):
    squares = size // PLACES
    if (
        size == PLACES * squares
        and squares > 1
        and squares & (squares - 1) == 0
        and fast_weights.shape[2] % squares == 0
    ):
        return square_body(
            queries, key_vectors, value_vectors, token_rates, fast_weights, squares
        )
    return gather_body(queries, key_vectors, value_vectors, token_rates, fast_weights)


def solution(mesh):
    in_specs = (
        P(("groups", "seq"), None),
        P(("groups", "seq"), None),
        P(("groups", "seq"), None),
        P(("groups", "seq"), None),
        P(("groups", "seq"), None, None, None),
    )
    out_specs = (P(("groups", "seq"), None), P(("groups", "seq"), None, None, None))
    return jax.shard_map(
        functools.partial(body, mesh.shape["seq"]),
        mesh=mesh,
        in_specs=in_specs,
        out_specs=out_specs,
        check_vma=False,
    )
```

```python
import functools
import math

import jax
import jax.numpy as jnp
from jax import lax
from jax.experimental import pallas as pl
from jax.experimental.pallas import tpu as pltpu
from jax.sharding import PartitionSpec as P

HID = 512
NS_STEPS = 2
PLACES = 4

coef_a = 3.4445
coef_b = -4.775
coef_c = 2.0315

VMEM = pltpu.VMEM
SMEM = pltpu.SMEM
NT = (((1,), (1,)), ((), ()))
NN = (((1,), (0,)), ((), ()))
TN = (((0,), (0,)), ((), ()))


def dot(a, b, dims, precision=None):
    return lax.dot_general(a, b, dims, precision=precision, preferred_element_type=jnp.float32)


def split_kernel(where_ref, q_ref, k_ref, v_ref, rate_ref, *refs):
    outs, scaled = refs[:-1], refs[-1]
    spot = where_ref[0]
    squares = len(outs) // 2
    width = outs[0].shape[2]
    num_heads = rate_ref.shape[1]
    head_size = k_ref.shape[1] // num_heads
    rates = (-1.0 / math.sqrt(HID)) * rate_ref[...]
    for head in range(num_heads):
        at = slice(head * head_size, (head + 1) * head_size)
        scaled[:, at] = (rates[:, head : head + 1] * v_ref[:, at].astype(jnp.float32)).astype(
            jnp.bfloat16
        )
    for rel in range(squares):
        at = pl.multiple_of((spot ^ rel) * width, width)
        outs[rel][0] = k_ref[:, pl.ds(at, width)]
        outs[rel][1] = scaled[:, pl.ds(at, width)]
        outs[squares + rel][...] = q_ref[:, pl.ds(at, width)]


def join_kernel(where_ref, *refs):
    ins, out_ref = refs[:-1], refs[-1]
    spot = where_ref[0]
    width = ins[0].shape[1]
    for rel, in_ref in enumerate(ins):
        at = pl.multiple_of((spot ^ rel) * width, width)
        out_ref[:, pl.ds(at, width)] = in_ref[...]


def weight_rows(w_refs, rel, matrix):
    pieces = w_refs[2 * rel : 2 * rel + 2]
    return jnp.concatenate(
        [w[at, 0, matrix] for w in pieces for at in range(w.shape[0])], axis=0
    )


def key_kernel(squares, heads, where_ref, *refs):
    pairs, w_refs = refs[:squares], refs[squares : squares + 8]
    mine_ref, sent_ref, near_ref, *far_refs, terms = refs[squares + 8 :]
    spot, place = where_ref[0], where_ref[1]
    _, hid, head_size = terms.shape
    rows = hid // (PLACES * squares)
    step = pl.program_id(0)
    scale_in = 1.0 / math.sqrt(head_size)

    def put(number, value):
        rel = (number % PLACES) ^ place
        slot = number // PLACES

        @pl.when(rel == 0)
        def _():
            mine_ref[slot] = value

        @pl.when(rel == 2)
        def _():
            sent_ref[slot] = value

        @pl.when(rel == 1)
        def _():
            near_ref[slot] = value.astype(near_ref.dtype)

        for one, far_ref in enumerate(far_refs):

            @pl.when((rel == 3) & (slot == one))
            def _():
                far_ref[...] = value.astype(far_ref.dtype)

    @pl.when(step == 0)
    def _():
        for number in range(3 * heads, PLACES * mine_ref.shape[0]):
            put(number, jnp.zeros((hid, head_size), jnp.float32))

    keys = jnp.concatenate([pair[0] for pair in pairs], axis=0)
    scaled = jnp.concatenate([pair[1] for pair in pairs], axis=0)
    both_maps = jnp.concatenate(
        [weight_rows(w_refs, rel, matrix) for matrix in range(2) for rel in range(PLACES)], axis=0
    )
    second = jnp.concatenate([weight_rows(w_refs, rel, 2) for rel in range(PLACES)], axis=0)
    raw = dot(both_maps, keys, NT)
    third = raw[hid:] * scale_in
    back = dot(second, scaled, NT)
    half_first = raw[:hid] * (0.5 * scale_in)
    tanh = jnp.tanh(half_first)
    act = half_first + half_first * tanh
    hidden = (act * third).astype(jnp.bfloat16)
    grad_third = (back * act).astype(jnp.bfloat16)
    twice_slope = (1.0 + tanh) + act * (1.0 - tanh)
    grad_first = (back * third * twice_slope).astype(jnp.bfloat16)
    firsts = dot(jnp.concatenate([grad_first, grad_third], axis=0), keys, NN)
    values = (
        firsts[:hid] * (0.5 * scale_in),
        firsts[hid:] * scale_in,
        dot(hidden, scaled, NN),
    )
    for rel in range(PLACES):
        for apart in range(squares):
            at = (rel * squares + apart) * rows
            to = pl.multiple_of(((place ^ rel) * squares + (spot ^ apart)) * rows, rows)
            for matrix in range(3):
                terms[matrix, pl.ds(to, rows), :] = values[matrix][at : at + rows]
    for matrix in range(3):
        put(3 * step + matrix, terms[matrix])


def query_kernel(squares, *refs):
    ins, w_refs, outs = refs[:squares], refs[squares : squares + 8], refs[-squares:]
    scale_in = 1.0 / math.sqrt(ins[0].shape[1])
    scale_out = 1.0 / math.sqrt(HID)
    first_map, third_map, second = (
        jnp.concatenate([weight_rows(w_refs, rel, matrix) for rel in range(PLACES)], axis=0)
        for matrix in range(3)
    )
    queries = jnp.concatenate([q_ref[...] for q_ref in ins], axis=0)
    half_first = dot(queries, first_map, NT) * (0.5 * scale_in)
    third = dot(queries, third_map, NT) * scale_in
    hidden = ((half_first + half_first * jnp.tanh(half_first)) * third).astype(jnp.bfloat16)
    out = (dot(hidden, second, NN) * scale_out).astype(jnp.bfloat16)
    rows = outs[0].shape[0]
    for rel, out_ref in enumerate(outs):
        out_ref[...] = out[rel * rows : (rel + 1) * rows]


def halves(array):
    high = array.astype(jnp.bfloat16)
    return high, (array - high.astype(jnp.float32)).astype(jnp.bfloat16)


def dot_halves(a, b, dims):
    return dot(a[0], b[0], dims) + (dot(a[0], b[1], dims) + dot(a[1], b[0], dims))


def pick_kernel(squares, where_ref, *refs):
    w_refs, out_ref = refs[:8], refs[8]
    spot, place = where_ref[0], where_ref[1]
    heads = w_refs[0].shape[1]
    for slot in range(out_ref.shape[1]):
        number = jnp.minimum(PLACES * slot + place, 3 * heads - 1)
        for rel in range(PLACES):
            owner = place ^ rel
            for apart in range(squares):
                w = w_refs[2 * rel + apart // (squares // 2)]
                to = device_of(owner, spot ^ apart, squares)
                out_ref[to, slot] = w[apart % (squares // 2), number // 3, number % 3]


def device_of(place, spot, squares):
    up = place // 2
    return (up * squares + (spot ^ up * (squares // 2))) * 2 + place % 2


def renew_kernel(squares, mine_ref, far_ref, old_ref, out_ref, updates):
    slots, hid, head_size = far_ref.shape
    rows = out_ref.shape[2]
    eye = (
        lax.broadcasted_iota(jnp.int32, (head_size, head_size), 0)
        == lax.broadcasted_iota(jnp.int32, (head_size, head_size), 1)
    ).astype(jnp.float32)
    grads = [
        mine_ref[slot]
        + far_ref[slot].astype(jnp.float32)
        for slot in range(slots)
    ]
    grads = [halves(grad) for grad in grads]
    grams = []
    for high, low in grads:
        cross = dot(high, low, TN)
        grams.append(dot(high, high, TN) + (cross + cross.T))
    scales = [1.0 / (jnp.sqrt(jnp.sum(gram * eye)) + 1e-07) for gram in grams]
    factors = []
    for gram, scale in zip(grams, scales):
        square = (scale * scale) * gram
        parts = halves(square)
        factors.append(
            scale * (coef_a * eye + coef_b * square + coef_c * dot_halves(parts, parts, NN))
        )
    grams = [halves(gram) for gram in grams]
    for _ in range(NS_STEPS - 1):
        parts = [halves(factor) for factor in factors]
        inner = [dot_halves(gram, part, NN) for gram, part in zip(grams, parts)]
        squares_of = [dot_halves(part, halves(term), NN) for part, term in zip(parts, inner)]
        mixed = []
        for square in squares_of:
            term = halves(square)
            mixed.append(coef_b * square + coef_c * dot_halves(term, term, NN))
        factors = [
            coef_a * factor + dot_halves(halves(term), part, NN)
            for term, factor, part in zip(mixed, factors, parts)
        ]
    for slot in range(slots):
        updates[slot] = math.sqrt(HID) * dot_halves(grads[slot], halves(factors[slot]), NT)
    for slot in range(slots):
        for owner in range(PLACES):
            for at in range(squares):
                to = device_of(owner, at, squares)
                rows_at = slice((owner * squares + at) * rows, (owner * squares + at + 1) * rows)
                old = old_ref[to, slot].astype(jnp.float32)
                out_ref[to, slot] = (old - updates[slot, rows_at, :]).astype(out_ref.dtype)


def square_body(queries, key_vectors, value_vectors, token_rates, fast_weights, squares):
    row_count = queries.shape[0]
    own_rows, _, num_heads, head_size = fast_weights.shape
    heads = num_heads // squares
    width = heads * head_size
    size = squares * PLACES
    half = size // 2
    hid = size * own_rows
    cut = squares // 2
    position = lax.axis_index("seq").astype(jnp.int32)
    turn = squares // 2
    spot = position % half // 2 ^ turn * (position // half)
    where = jnp.stack([spot, 2 * (position // half) + position % 2])
    partner = half + 2 * turn
    params = pltpu.CompilerParams(vmem_limit_bytes=40 * 2**20)
    smem = pl.BlockSpec(memory_space=SMEM)
    vmem = pl.BlockSpec(memory_space=VMEM)

    def cost(mega_flops):
        return pl.CostEstimate(
            flops=mega_flops * 10**6, bytes_accessed=4 * 10**6, transcendentals=0
        )

    def swap(array, step):
        return lax.ppermute(array, "seq", [(at, at ^ step) for at in range(size)])

    def across(pieces):
        return [pieces[0]] + [swap(pieces[rel], 2 * rel) for rel in range(1, squares)]

    def bf16(*shape):
        return jax.ShapeDtypeStruct(shape, jnp.bfloat16)

    pieces = pl.pallas_call(
        split_kernel,
        in_specs=[smem] + [vmem] * 4,
        out_specs=[vmem] * (2 * squares),
        out_shape=[bf16(2, row_count, width)] * squares + [bf16(row_count, width)] * squares,
        scratch_shapes=[VMEM((row_count, num_heads * head_size), jnp.bfloat16)],
        compiler_params=params,
        cost_estimate=cost(10),
        name="split",
    )(where, queries, key_vectors, value_vectors, token_rates)
    moved, asking = across(pieces[:squares]), pieces[squares:]

    by_spot = fast_weights.reshape(own_rows, 3, squares, heads, head_size).transpose(2, 3, 1, 0, 4)
    pieces = across(
        [
            lax.dynamic_index_in_dim(by_spot, spot ^ rel, 0, keepdims=False)
            for rel in range(squares)
        ]
    )
    own = [jnp.stack(pieces[:cut]), jnp.stack(pieces[cut:])]
    own = list(lax.optimization_barrier(own))
    other = [swap(w, partner) for w in own]
    late, moved[2:] = lax.optimization_barrier((other, moved[2:]))
    other, asking = lax.optimization_barrier((other, asking))
    asking = across(asking)
    weights = [own, [swap(w, 1) for w in own], other, [swap(w, 1) for w in late]]
    weights = [w for pair in weights for w in pair]

    weight_spec = pl.BlockSpec((cut, 1, 3, own_rows, head_size), lambda h: (0, h, 0, 0, 0))

    slots = -(-3 * heads // PLACES)
    sums_shape = (slots, hid, head_size)
    mine, sent, near, *far = pl.pallas_call(
        functools.partial(key_kernel, squares, heads),
        grid=(heads,),
        in_specs=[smem]
        + [pl.BlockSpec((2, row_count, head_size), lambda h: (0, 0, h))] * squares
        + [weight_spec] * 8,
        out_specs=[pl.BlockSpec(sums_shape, lambda h: (0, 0, 0))] * 3
        + [pl.BlockSpec(sums_shape[1:], lambda h: (0, 0))] * slots,
        out_shape=[
            jax.ShapeDtypeStruct(sums_shape, jnp.float32),
            jax.ShapeDtypeStruct(sums_shape, jnp.float32),
            bf16(*sums_shape),
            *[bf16(*sums_shape[1:])] * slots,
        ],
        scratch_shapes=[VMEM((3, hid, head_size), jnp.float32)],
        compiler_params=params,
        cost_estimate=cost(2000),
        name="key_side",
    )(where, *moved, *weights)

    near = swap(near, 1)
    mine = mine + near.astype(jnp.float32)
    far = [swap(one, 1) for one in far]
    far, asking = lax.optimization_barrier((far, asking))
    far = jnp.stack(far).astype(jnp.float32)
    far = swap((sent + far).astype(jnp.bfloat16), partner)

    columns = pl.BlockSpec((row_count, head_size), lambda h: (0, h))
    parts = pl.pallas_call(
        functools.partial(query_kernel, squares),
        grid=(heads,),
        in_specs=[columns] * squares
        + [weight_spec] * 8,
        out_specs=[columns] * squares,
        out_shape=[bf16(row_count, width)] * squares,
        compiler_params=params,
        cost_estimate=cost(1000),
        name="query_side",
    )(*asking, *weights)
    parts, late_weights = lax.optimization_barrier((parts, weights))
    parts = across(parts)
    far, parts[2:] = lax.optimization_barrier((far, parts[2:]))
    applied = pl.pallas_call(
        join_kernel,
        in_specs=[smem] + [vmem] * squares,
        out_specs=vmem,
        out_shape=bf16(row_count, num_heads * head_size),
        compiler_params=params,
        cost_estimate=cost(10),
        name="join",
    )(where, *parts)

    old = pl.pallas_call(
        functools.partial(pick_kernel, squares),
        in_specs=[smem] + [vmem] * 8,
        out_specs=vmem,
        out_shape=bf16(size, slots, own_rows, head_size),
        compiler_params=params,
        cost_estimate=cost(10),
        name="pick",
    )(where, *late_weights)
    renewed = pl.pallas_call(
        functools.partial(renew_kernel, squares),
        in_specs=[vmem] * 3,
        out_specs=vmem,
        out_shape=bf16(size, slots, own_rows, head_size),
        scratch_shapes=[VMEM(sums_shape, jnp.float32)],
        compiler_params=params,
        cost_estimate=cost(2000),
        name="renew",
    )(mine, far, old)
    back = lax.all_to_all(renewed, "seq", 0, 0, tiled=True)
    back = back.reshape(2, squares, 2, slots, own_rows, head_size)
    back = jnp.stack([back[0], jnp.roll(back[1], turn, axis=0)])
    back = back.transpose(1, 3, 0, 2, 4, 5)
    back = back.reshape(squares, PLACES * slots, own_rows, head_size)[:, : 3 * heads]
    renewed_out = (
        back.reshape(squares, heads, 3, own_rows, head_size)
        .transpose(3, 2, 0, 1, 4)
        .reshape(own_rows, 3, num_heads, head_size)
    )
    return applied, renewed_out


def newton_factor(gram_matrix):
    exact = lax.Precision.HIGHEST
    head_size = gram_matrix.shape[-1]
    trace_sum = jnp.trace(gram_matrix, axis1=-2, axis2=-1)
    factor = 1.0 / (jnp.sqrt(trace_sum) + 1e-07)
    poly_factor = factor[..., None, None] * jnp.eye(head_size, dtype=jnp.float32)
    for newton_step in range(NS_STEPS):
        inner_term = jnp.matmul(gram_matrix, poly_factor, precision=exact)
        square = jnp.matmul(poly_factor, inner_term, precision=exact)
        mixed_term = coef_b * square + coef_c * jnp.matmul(square, square, precision=exact)
        poly_factor = coef_a * poly_factor + jnp.matmul(mixed_term, poly_factor, precision=exact)
    return poly_factor


def hidden_block(query_heads, key_heads, scaled_v, weight_block):
    head_size = query_heads.shape[2]
    scale_in = 1.0 / math.sqrt(head_size)
    scale_out = 1.0 / math.sqrt(HID)
    query_first = scale_in * jnp.einsum(
        "thd,jhd->thj", query_heads, weight_block[:, 0], preferred_element_type=jnp.float32
    )
    query_third = scale_in * jnp.einsum(
        "thd,jhd->thj", query_heads, weight_block[:, 1], preferred_element_type=jnp.float32
    )
    hidden_q = (query_first * jax.nn.sigmoid(query_first) * query_third).astype(jnp.bfloat16)
    partial_out = scale_out * jnp.einsum(
        "thj,jhd->thd", hidden_q, weight_block[:, 2], preferred_element_type=jnp.float32
    )
    key_first = scale_in * jnp.einsum(
        "thd,jhd->thj", key_heads, weight_block[:, 0], preferred_element_type=jnp.float32
    )
    key_third = scale_in * jnp.einsum(
        "thd,jhd->thj", key_heads, weight_block[:, 1], preferred_element_type=jnp.float32
    )
    sigmoid_k = jax.nn.sigmoid(key_first)
    activated = key_first * sigmoid_k
    hidden_k = (activated * key_third).astype(jnp.bfloat16)
    back_grad = jnp.einsum(
        "thd,jhd->thj", scaled_v, weight_block[:, 2], preferred_element_type=jnp.float32
    )
    grad_third = (back_grad * activated).astype(jnp.bfloat16)
    grad_first = (back_grad * key_third * sigmoid_k * (1.0 + key_first * (1.0 - sigmoid_k))).astype(
        jnp.bfloat16
    )
    return (partial_out, hidden_k, grad_first, grad_third)


def gather_body(queries, key_vectors, value_vectors, token_rates, fast_weights):
    exact = lax.Precision.HIGHEST
    row_count = queries.shape[0]
    num_heads = fast_weights.shape[2]
    head_size = fast_weights.shape[3]
    scale_in = 1.0 / math.sqrt(head_size)
    scale_out = 1.0 / math.sqrt(HID)
    query_heads = queries.reshape(row_count, num_heads, head_size)
    key_heads = key_vectors.reshape(row_count, num_heads, head_size)
    value_heads = value_vectors.reshape(row_count, num_heads, head_size)
    scaled_v = (-scale_out * token_rates[:, :, None] * value_heads.astype(jnp.float32)).astype(
        jnp.bfloat16
    )
    gathered = lax.all_gather(fast_weights, "seq", axis=0, tiled=True)
    out_sum, hidden_k, grad_first, grad_third = hidden_block(
        query_heads, key_heads, scaled_v, gathered
    )
    applied = out_sum.astype(jnp.bfloat16).reshape(row_count, num_heads * head_size)
    terms = (
        scale_in
        * jnp.einsum("thj,thd->jhd", grad_first, key_heads, preferred_element_type=jnp.float32),
        scale_in
        * jnp.einsum("thj,thd->jhd", grad_third, key_heads, preferred_element_type=jnp.float32),
        jnp.einsum("thj,thd->jhd", hidden_k, scaled_v, preferred_element_type=jnp.float32),
    )
    sums = [
        jnp.sum(
            lax.all_to_all(term[:, None], "seq", split_axis=0, concat_axis=1, tiled=True), axis=1
        )
        for term in terms
    ]
    gradient = jnp.stack(sums, axis=1)
    partial_gram = jnp.einsum("jmhd,jmhe->mhde", gradient, gradient, precision=exact)
    gram_matrix = lax.psum(partial_gram, "seq")
    poly_factor = newton_factor(gram_matrix)
    update = jnp.einsum("mhde,jmhe->jmhd", poly_factor, gradient, precision=exact)
    renewed = (fast_weights.astype(jnp.float32) - math.sqrt(HID) * update).astype(jnp.bfloat16)
    return (applied, renewed)


def body(size, queries, key_vectors, value_vectors, token_rates, fast_weights):
    squares = size // PLACES
    if (
        size == PLACES * squares
        and squares > 1
        and squares & (squares - 1) == 0
        and fast_weights.shape[2] % squares == 0
    ):
        return square_body(
            queries, key_vectors, value_vectors, token_rates, fast_weights, squares
        )
    return gather_body(queries, key_vectors, value_vectors, token_rates, fast_weights)


def solution(mesh):
    in_specs = (
        P(("groups", "seq"), None),
        P(("groups", "seq"), None),
        P(("groups", "seq"), None),
        P(("groups", "seq"), None),
        P(("groups", "seq"), None, None, None),
    )
    out_specs = (P(("groups", "seq"), None), P(("groups", "seq"), None, None, None))
    return jax.shard_map(
        functools.partial(body, mesh.shape["seq"]),
        mesh=mesh,
        in_specs=in_specs,
        out_specs=out_specs,
        check_vma=False,
    )
```

```python
import functools
import math

import jax
import jax.numpy as jnp
from jax import lax
from jax.experimental import pallas as pl
from jax.experimental.pallas import tpu as pltpu
from jax.sharding import PartitionSpec as P

HID = 512
NS_STEPS = 2
PLACES = 4

coef_a = 3.4445
coef_b = -4.775
coef_c = 2.0315

VMEM = pltpu.VMEM
SMEM = pltpu.SMEM
NT = (((1,), (1,)), ((), ()))
NN = (((1,), (0,)), ((), ()))
TN = (((0,), (0,)), ((), ()))


def dot(a, b, dims, precision=None):
    return lax.dot_general(a, b, dims, precision=precision, preferred_element_type=jnp.float32)


def split_kernel(where_ref, q_ref, k_ref, v_ref, rate_ref, *refs):
    outs, scaled = refs[:-1], refs[-1]
    spot = where_ref[0]
    squares = len(outs) // 2
    width = outs[0].shape[2]
    num_heads = rate_ref.shape[1]
    head_size = k_ref.shape[1] // num_heads
    rates = (-1.0 / math.sqrt(HID)) * rate_ref[...]
    for head in range(num_heads):
        at = slice(head * head_size, (head + 1) * head_size)
        scaled[:, at] = (rates[:, head : head + 1] * v_ref[:, at].astype(jnp.float32)).astype(
            jnp.bfloat16
        )
    for rel in range(squares):
        at = pl.multiple_of((spot ^ rel) * width, width)
        outs[rel][0] = k_ref[:, pl.ds(at, width)]
        outs[rel][1] = scaled[:, pl.ds(at, width)]
        outs[squares + rel][...] = q_ref[:, pl.ds(at, width)]


def join_kernel(where_ref, *refs):
    ins, out_ref = refs[:-1], refs[-1]
    spot = where_ref[0]
    width = ins[0].shape[1]
    for rel, in_ref in enumerate(ins):
        at = pl.multiple_of((spot ^ rel) * width, width)
        out_ref[:, pl.ds(at, width)] = in_ref[...]


def weight_rows(w_refs, rel, matrix):
    pieces = w_refs[2 * rel : 2 * rel + 2]
    return jnp.concatenate(
        [w[at, 0, matrix] for w in pieces for at in range(w.shape[0])], axis=0
    )


def key_kernel(squares, heads, where_ref, *refs):
    pairs, w_refs = refs[:squares], refs[squares : squares + 8]
    mine_ref, sent_ref, near_ref, *far_refs, terms = refs[squares + 8 :]
    spot, place = where_ref[0], where_ref[1]
    _, hid, head_size = terms.shape
    rows = hid // (PLACES * squares)
    step = pl.program_id(0)
    scale_in = 1.0 / math.sqrt(head_size)

    def put(number, value):
        rel = (number % PLACES) ^ place
        slot = number // PLACES

        @pl.when(rel == 0)
        def _():
            mine_ref[slot] = value

        @pl.when(rel == 2)
        def _():
            sent_ref[slot] = value

        @pl.when(rel == 1)
        def _():
            near_ref[slot] = value.astype(near_ref.dtype)

        for one, far_ref in enumerate(far_refs):

            @pl.when((rel == 3) & (slot == one))
            def _():
                far_ref[...] = value.astype(far_ref.dtype)

    @pl.when(step == 0)
    def _():
        for number in range(3 * heads, PLACES * mine_ref.shape[0]):
            put(number, jnp.zeros((hid, head_size), jnp.float32))

    keys = jnp.concatenate([pair[0] for pair in pairs], axis=0)
    scaled = jnp.concatenate([pair[1] for pair in pairs], axis=0)
    both_maps = jnp.concatenate(
        [weight_rows(w_refs, rel, matrix) for matrix in range(2) for rel in range(PLACES)], axis=0
    )
    second = jnp.concatenate([weight_rows(w_refs, rel, 2) for rel in range(PLACES)], axis=0)
    raw = dot(both_maps, keys, NT)
    third = raw[hid:] * scale_in
    back = dot(second, scaled, NT)
    half_first = raw[:hid] * (0.5 * scale_in)
    tanh = jnp.tanh(half_first)
    act = half_first + half_first * tanh
    hidden = (act * third).astype(jnp.bfloat16)
    grad_third = (back * act).astype(jnp.bfloat16)
    twice_slope = (1.0 + tanh) + act * (1.0 - tanh)
    grad_first = (back * third * twice_slope).astype(jnp.bfloat16)
    firsts = dot(jnp.concatenate([grad_first, grad_third], axis=0), keys, NN)
    values = (
        firsts[:hid] * (0.5 * scale_in),
        firsts[hid:] * scale_in,
        dot(hidden, scaled, NN),
    )
    for rel in range(PLACES):
        for apart in range(squares):
            at = (rel * squares + apart) * rows
            to = pl.multiple_of(((place ^ rel) * squares + (spot ^ apart)) * rows, rows)
            for matrix in range(3):
                terms[matrix, pl.ds(to, rows), :] = values[matrix][at : at + rows]
    for matrix in range(3):
        put(3 * step + matrix, terms[matrix])


def query_kernel(squares, *refs):
    ins, w_refs, outs = refs[:squares], refs[squares : squares + 8], refs[-squares:]
    scale_in = 1.0 / math.sqrt(ins[0].shape[1])
    scale_out = 1.0 / math.sqrt(HID)
    first_map, third_map, second = (
        jnp.concatenate([weight_rows(w_refs, rel, matrix) for rel in range(PLACES)], axis=0)
        for matrix in range(3)
    )
    queries = jnp.concatenate([q_ref[...] for q_ref in ins], axis=0)
    half_first = dot(queries, first_map, NT) * (0.5 * scale_in)
    third = dot(queries, third_map, NT) * scale_in
    hidden = ((half_first + half_first * jnp.tanh(half_first)) * third).astype(jnp.bfloat16)
    out = (dot(hidden, second, NN) * scale_out).astype(jnp.bfloat16)
    rows = outs[0].shape[0]
    for rel, out_ref in enumerate(outs):
        out_ref[...] = out[rel * rows : (rel + 1) * rows]


def halves(array):
    high = array.astype(jnp.bfloat16)
    return high, (array - high.astype(jnp.float32)).astype(jnp.bfloat16)


def dot_halves(a, b, dims):
    return dot(a[0], b[0], dims) + (dot(a[0], b[1], dims) + dot(a[1], b[0], dims))


def pick_kernel(squares, where_ref, *refs):
    w_refs, out_ref = refs[:8], refs[8]
    spot, place = where_ref[0], where_ref[1]
    heads = w_refs[0].shape[1]
    for slot in range(out_ref.shape[1]):
        number = jnp.minimum(PLACES * slot + place, 3 * heads - 1)
        for rel in range(PLACES):
            owner = place ^ rel
            for apart in range(squares):
                w = w_refs[2 * rel + apart // (squares // 2)]
                to = device_of(owner, spot ^ apart, squares)
                out_ref[to, slot] = w[apart % (squares // 2), number // 3, number % 3]


def device_of(place, spot, squares):
    up = place // 2
    return (up * squares + (spot ^ up * (squares // 2))) * 2 + place % 2


def renew_kernel(squares, mine_ref, far_ref, old_ref, out_ref, updates):
    slots, hid, head_size = far_ref.shape
    rows = out_ref.shape[2]
    eye = (
        lax.broadcasted_iota(jnp.int32, (head_size, head_size), 0)
        == lax.broadcasted_iota(jnp.int32, (head_size, head_size), 1)
    ).astype(jnp.float32)
    grads = [
        mine_ref[slot]
        + far_ref[slot].astype(jnp.float32)
        for slot in range(slots)
    ]
    grads = [halves(grad) for grad in grads]
    grams = []
    for high, low in grads:
        cross = dot(high, low, TN)
        grams.append(dot(high, high, TN) + (cross + cross.T))
    scales = [1.0 / (jnp.sqrt(jnp.sum(gram * eye)) + 1e-07) for gram in grams]
    factors = []
    for gram, scale in zip(grams, scales):
        square = (scale * scale) * gram
        parts = halves(square)
        factors.append(
            scale * (coef_a * eye + coef_b * square + coef_c * dot_halves(parts, parts, NN))
        )
    grams = [halves(gram) for gram in grams]
    for _ in range(NS_STEPS - 1):
        parts = [halves(factor) for factor in factors]
        inner = [dot_halves(gram, part, NN) for gram, part in zip(grams, parts)]
        squares_of = [dot_halves(part, halves(term), NN) for part, term in zip(parts, inner)]
        mixed = []
        for square in squares_of:
            term = halves(square)
            mixed.append(coef_b * square + coef_c * dot_halves(term, term, NN))
        factors = [
            coef_a * factor + dot_halves(halves(term), part, NN)
            for term, factor, part in zip(mixed, factors, parts)
        ]
    for slot in range(slots):
        updates[slot] = math.sqrt(HID) * dot_halves(grads[slot], halves(factors[slot]), NT)
    for slot in range(slots):
        for owner in range(PLACES):
            for at in range(squares):
                to = device_of(owner, at, squares)
                rows_at = slice((owner * squares + at) * rows, (owner * squares + at + 1) * rows)
                old = old_ref[to, slot].astype(jnp.float32)
                out_ref[to, slot] = (old - updates[slot, rows_at, :]).astype(out_ref.dtype)


def square_body(queries, key_vectors, value_vectors, token_rates, fast_weights, squares):
    row_count = queries.shape[0]
    own_rows, _, num_heads, head_size = fast_weights.shape
    heads = num_heads // squares
    width = heads * head_size
    size = squares * PLACES
    half = size // 2
    hid = size * own_rows
    cut = squares // 2
    position = lax.axis_index("seq").astype(jnp.int32)
    turn = squares // 2
    spot = position % half // 2 ^ turn * (position // half)
    where = jnp.stack([spot, 2 * (position // half) + position % 2])
    partner = half + 2 * turn
    params = pltpu.CompilerParams(vmem_limit_bytes=40 * 2**20)
    smem = pl.BlockSpec(memory_space=SMEM)
    vmem = pl.BlockSpec(memory_space=VMEM)

    def cost(mega_flops):
        return pl.CostEstimate(
            flops=mega_flops * 10**6, bytes_accessed=4 * 10**6, transcendentals=0
        )

    def swap(array, step):
        return lax.ppermute(array, "seq", [(at, at ^ step) for at in range(size)])

    def across(pieces):
        return [pieces[0]] + [swap(pieces[rel], 2 * rel) for rel in range(1, squares)]

    def bf16(*shape):
        return jax.ShapeDtypeStruct(shape, jnp.bfloat16)

    pieces = pl.pallas_call(
        split_kernel,
        in_specs=[smem] + [vmem] * 4,
        out_specs=[vmem] * (2 * squares),
        out_shape=[bf16(2, row_count, width)] * squares + [bf16(row_count, width)] * squares,
        scratch_shapes=[VMEM((row_count, num_heads * head_size), jnp.bfloat16)],
        compiler_params=params,
        cost_estimate=cost(10),
        name="split",
    )(where, queries, key_vectors, value_vectors, token_rates)
    moved, asking = across(pieces[:squares]), pieces[squares:]

    by_spot = fast_weights.reshape(own_rows, 3, squares, heads, head_size).transpose(2, 3, 1, 0, 4)
    pieces = across(
        [
            lax.dynamic_index_in_dim(by_spot, spot ^ rel, 0, keepdims=False)
            for rel in range(squares)
        ]
    )
    own = [jnp.stack(pieces[:cut]), jnp.stack(pieces[cut:])]
    own = list(lax.optimization_barrier(own))
    other = [swap(w, partner) for w in own]
    late, moved[2:] = lax.optimization_barrier((other, moved[2:]))
    moved[2:], asking = lax.optimization_barrier((moved[2:], asking))
    asking = across(asking)
    weights = [own, [swap(w, 1) for w in own], other, [swap(w, 1) for w in late]]
    weights = [w for pair in weights for w in pair]

    weight_spec = pl.BlockSpec((cut, 1, 3, own_rows, head_size), lambda h: (0, h, 0, 0, 0))

    slots = -(-3 * heads // PLACES)
    sums_shape = (slots, hid, head_size)
    mine, sent, near, *far = pl.pallas_call(
        functools.partial(key_kernel, squares, heads),
        grid=(heads,),
        in_specs=[smem]
        + [pl.BlockSpec((2, row_count, head_size), lambda h: (0, 0, h))] * squares
        + [weight_spec] * 8,
        out_specs=[pl.BlockSpec(sums_shape, lambda h: (0, 0, 0))] * 3
        + [pl.BlockSpec(sums_shape[1:], lambda h: (0, 0))] * slots,
        out_shape=[
            jax.ShapeDtypeStruct(sums_shape, jnp.float32),
            jax.ShapeDtypeStruct(sums_shape, jnp.float32),
            bf16(*sums_shape),
            *[bf16(*sums_shape[1:])] * slots,
        ],
        scratch_shapes=[VMEM((3, hid, head_size), jnp.float32)],
        compiler_params=params,
        cost_estimate=cost(2000),
        name="key_side",
    )(where, *moved, *weights)

    near = swap(near, 1)
    mine = mine + near.astype(jnp.float32)
    far = [swap(one, 1) for one in far]
    far, asking = lax.optimization_barrier((far, asking))
    far = jnp.stack(far).astype(jnp.float32)
    far = swap((sent + far).astype(jnp.bfloat16), partner)

    columns = pl.BlockSpec((row_count, head_size), lambda h: (0, h))
    parts = pl.pallas_call(
        functools.partial(query_kernel, squares),
        grid=(heads,),
        in_specs=[columns] * squares
        + [weight_spec] * 8,
        out_specs=[columns] * squares,
        out_shape=[bf16(row_count, width)] * squares,
        compiler_params=params,
        cost_estimate=cost(1000),
        name="query_side",
    )(*asking, *weights)
    parts, late_weights = lax.optimization_barrier((parts, weights))
    parts = across(parts)
    far, parts[2:] = lax.optimization_barrier((far, parts[2:]))
    applied = pl.pallas_call(
        join_kernel,
        in_specs=[smem] + [vmem] * squares,
        out_specs=vmem,
        out_shape=bf16(row_count, num_heads * head_size),
        compiler_params=params,
        cost_estimate=cost(10),
        name="join",
    )(where, *parts)

    old = pl.pallas_call(
        functools.partial(pick_kernel, squares),
        in_specs=[smem] + [vmem] * 8,
        out_specs=vmem,
        out_shape=bf16(size, slots, own_rows, head_size),
        compiler_params=params,
        cost_estimate=cost(10),
        name="pick",
    )(where, *late_weights)
    renewed = pl.pallas_call(
        functools.partial(renew_kernel, squares),
        in_specs=[vmem] * 3,
        out_specs=vmem,
        out_shape=bf16(size, slots, own_rows, head_size),
        scratch_shapes=[VMEM(sums_shape, jnp.float32)],
        compiler_params=params,
        cost_estimate=cost(2000),
        name="renew",
    )(mine, far, old)
    back = lax.all_to_all(renewed, "seq", 0, 0, tiled=True)
    back = back.reshape(2, squares, 2, slots, own_rows, head_size)
    back = jnp.stack([back[0], jnp.roll(back[1], turn, axis=0)])
    back = back.transpose(1, 3, 0, 2, 4, 5)
    back = back.reshape(squares, PLACES * slots, own_rows, head_size)[:, : 3 * heads]
    renewed_out = (
        back.reshape(squares, heads, 3, own_rows, head_size)
        .transpose(3, 2, 0, 1, 4)
        .reshape(own_rows, 3, num_heads, head_size)
    )
    return applied, renewed_out


def newton_factor(gram_matrix):
    exact = lax.Precision.HIGHEST
    head_size = gram_matrix.shape[-1]
    trace_sum = jnp.trace(gram_matrix, axis1=-2, axis2=-1)
    factor = 1.0 / (jnp.sqrt(trace_sum) + 1e-07)
    poly_factor = factor[..., None, None] * jnp.eye(head_size, dtype=jnp.float32)
    for newton_step in range(NS_STEPS):
        inner_term = jnp.matmul(gram_matrix, poly_factor, precision=exact)
        square = jnp.matmul(poly_factor, inner_term, precision=exact)
        mixed_term = coef_b * square + coef_c * jnp.matmul(square, square, precision=exact)
        poly_factor = coef_a * poly_factor + jnp.matmul(mixed_term, poly_factor, precision=exact)
    return poly_factor


def hidden_block(query_heads, key_heads, scaled_v, weight_block):
    head_size = query_heads.shape[2]
    scale_in = 1.0 / math.sqrt(head_size)
    scale_out = 1.0 / math.sqrt(HID)
    query_first = scale_in * jnp.einsum(
        "thd,jhd->thj", query_heads, weight_block[:, 0], preferred_element_type=jnp.float32
    )
    query_third = scale_in * jnp.einsum(
        "thd,jhd->thj", query_heads, weight_block[:, 1], preferred_element_type=jnp.float32
    )
    hidden_q = (query_first * jax.nn.sigmoid(query_first) * query_third).astype(jnp.bfloat16)
    partial_out = scale_out * jnp.einsum(
        "thj,jhd->thd", hidden_q, weight_block[:, 2], preferred_element_type=jnp.float32
    )
    key_first = scale_in * jnp.einsum(
        "thd,jhd->thj", key_heads, weight_block[:, 0], preferred_element_type=jnp.float32
    )
    key_third = scale_in * jnp.einsum(
        "thd,jhd->thj", key_heads, weight_block[:, 1], preferred_element_type=jnp.float32
    )
    sigmoid_k = jax.nn.sigmoid(key_first)
    activated = key_first * sigmoid_k
    hidden_k = (activated * key_third).astype(jnp.bfloat16)
    back_grad = jnp.einsum(
        "thd,jhd->thj", scaled_v, weight_block[:, 2], preferred_element_type=jnp.float32
    )
    grad_third = (back_grad * activated).astype(jnp.bfloat16)
    grad_first = (back_grad * key_third * sigmoid_k * (1.0 + key_first * (1.0 - sigmoid_k))).astype(
        jnp.bfloat16
    )
    return (partial_out, hidden_k, grad_first, grad_third)


def gather_body(queries, key_vectors, value_vectors, token_rates, fast_weights):
    exact = lax.Precision.HIGHEST
    row_count = queries.shape[0]
    num_heads = fast_weights.shape[2]
    head_size = fast_weights.shape[3]
    scale_in = 1.0 / math.sqrt(head_size)
    scale_out = 1.0 / math.sqrt(HID)
    query_heads = queries.reshape(row_count, num_heads, head_size)
    key_heads = key_vectors.reshape(row_count, num_heads, head_size)
    value_heads = value_vectors.reshape(row_count, num_heads, head_size)
    scaled_v = (-scale_out * token_rates[:, :, None] * value_heads.astype(jnp.float32)).astype(
        jnp.bfloat16
    )
    gathered = lax.all_gather(fast_weights, "seq", axis=0, tiled=True)
    out_sum, hidden_k, grad_first, grad_third = hidden_block(
        query_heads, key_heads, scaled_v, gathered
    )
    applied = out_sum.astype(jnp.bfloat16).reshape(row_count, num_heads * head_size)
    terms = (
        scale_in
        * jnp.einsum("thj,thd->jhd", grad_first, key_heads, preferred_element_type=jnp.float32),
        scale_in
        * jnp.einsum("thj,thd->jhd", grad_third, key_heads, preferred_element_type=jnp.float32),
        jnp.einsum("thj,thd->jhd", hidden_k, scaled_v, preferred_element_type=jnp.float32),
    )
    sums = [
        jnp.sum(
            lax.all_to_all(term[:, None], "seq", split_axis=0, concat_axis=1, tiled=True), axis=1
        )
        for term in terms
    ]
    gradient = jnp.stack(sums, axis=1)
    partial_gram = jnp.einsum("jmhd,jmhe->mhde", gradient, gradient, precision=exact)
    gram_matrix = lax.psum(partial_gram, "seq")
    poly_factor = newton_factor(gram_matrix)
    update = jnp.einsum("mhde,jmhe->jmhd", poly_factor, gradient, precision=exact)
    renewed = (fast_weights.astype(jnp.float32) - math.sqrt(HID) * update).astype(jnp.bfloat16)
    return (applied, renewed)


def body(size, queries, key_vectors, value_vectors, token_rates, fast_weights):
    squares = size // PLACES
    if (
        size == PLACES * squares
        and squares > 1
        and squares & (squares - 1) == 0
        and fast_weights.shape[2] % squares == 0
    ):
        return square_body(
            queries, key_vectors, value_vectors, token_rates, fast_weights, squares
        )
    return gather_body(queries, key_vectors, value_vectors, token_rates, fast_weights)


def solution(mesh):
    in_specs = (
        P(("groups", "seq"), None),
        P(("groups", "seq"), None),
        P(("groups", "seq"), None),
        P(("groups", "seq"), None),
        P(("groups", "seq"), None, None, None),
    )
    out_specs = (P(("groups", "seq"), None), P(("groups", "seq"), None, None, None))
    return jax.shard_map(
        functools.partial(body, mesh.shape["seq"]),
        mesh=mesh,
        in_specs=in_specs,
        out_specs=out_specs,
        check_vma=False,
    )
```
